512 devices in a mesh: pipe: 8 (over z_hi, y), expert: 64 (over z_lo, x, core).
Axes of the slice: x: 4, y: 4, z: 16 (z_hi: 2, z_lo: 8; z = z_hi * 8 + z_lo), core: 2. Of those that a mesh axis runs over, the one named last changes fastest.
Arguments:
- forward_state: bfloat16 [8, 4096, 3584], P('pipe', 'expert'), may hold values from -6 to 6
- grad_state: bfloat16 [8, 4096, 3584], P('pipe', 'expert'), may hold values from -6 to 6
- forward_routes: int32 [8, 4096, 1], P('pipe', 'expert'), may hold values from 0 to 7; in each aligned block of 64 rows (0 to 63, 64 to 127, ..., all dimensions but the last counted through in order) at most 8 rows name the same one
- forward_gates: bfloat16 [8, 4096, 1], P('pipe', 'expert'), may hold values from 0.19921875 to 2
- backward_routes: int32 [8, 4096, 1], P('pipe', 'expert'), may hold values from 0 to 7; in each aligned block of 64 rows (0 to 63, 64 to 127, ..., all dimensions but the last counted through in order) at most 8 rows name the same one
- backward_gates: bfloat16 [8, 4096, 1], P('pipe', 'expert'), may hold values from 0.19921875 to 2
- saved_preacts: bfloat16 [8, 2, 64, 8, 8192], P('pipe', None, None, None, 'expert'), may hold values from -6 to 6
- gate_weight: bfloat16 [8, 3584, 8192], P('pipe', None, 'expert'), may hold values from -0.09375 to 0.09375
- up_weight: bfloat16 [8, 3584, 8192], P('pipe', None, 'expert'), may hold values from -0.09375 to 0.09375
- down_weight: bfloat16 [8, 8192, 3584], P('pipe', 'expert'), may hold values from -0.1875 to 0.1875
Outputs:
- forward_next: bfloat16 [8, 4096, 3584], P('pipe', 'expert')
- backward_next: bfloat16 [8, 4096, 3584], P('pipe', 'expert')
The draws below stay inside these ranges and needn't reach their ends.
Inputs may be any that keep to these rules, and one draw needn't show every extreme that they name: `forward_routes`: in the 64 tokens of one device at one section, every expert is named by exactly 8 (token, choice) pairs; the 1 expert of a token differ. `backward_routes`: in the 64 tokens of one device at one section, every expert is named by exactly 8 (token, choice) pairs; the 1 expert of a token differ.
All inputs are finite; a program needn't handle non-finite values.
Results may differ from the reference program's by a relative error of at most 0.011.
Values may be sent and summed in bfloat16 or wider, within the bound.
No kernel may reach another device: no remote copies, remote signals or barrier semaphores. Data moves between devices by JAX's collectives and lax.ppermute only.
A program may use at most 128 MiB of HBM per device.

```python
import math
from functools import partial
import jax
import jax.numpy as jnp
import numpy as np
from jax import lax

D = 3584
FF = 1024
TOP = 1
WSPLIT = 8
TOK_DEV = 64
SECTIONS = 8
SOURCES = 64
EXPERTS = 8
FF_DEV = 128
CAP = 8
TOKENS = 4096


def block_levels(stream_key, dims, split, smallest, largest):
    loudness, own = 1.0, jax.random.fold_in(stream_key, 6)
    for dim, blocks in split:
        steps = jnp.exp(jax.random.uniform(jax.random.fold_in(own, dim), (blocks,), jnp.float32, smallest / len(split), largest / len(split)))
        loudness = loudness * jnp.repeat(steps, dims[dim] // blocks).reshape([-1 if axis == dim else 1 for axis in range(len(dims))])
    return loudness


def assign_block(own_key, own, number, rows, amount, top, most, lean):
    order = jax.random.permutation(own_key, amount)
    crowded, common = portions_of(amount, rows * top, most, lean, True), portions_of(amount, rows * top, most, lean, False)
    places = jnp.arange(amount)

    def named(tallies, turn):
        used = int((tallies > 0).sum())
        fixed = max(1, used // 4)
        shifted = fixed + (places - fixed + turn * (used - fixed)) % max(1, amount - fixed)
        return jnp.zeros((amount,), jnp.int32).at[order[jnp.where(places < fixed, places, shifted)]].set(jnp.asarray(tallies, jnp.int32))

    tallies = jnp.where(number % 4 == 0, named(crowded, number // 4), named(common, number - number // 4 - 1))
    mixed = jax.random.permutation(jax.random.fold_in(own, 3), amount)
    source_of, receiver = mixed[0:amount // 2 * 2:2], mixed[1:amount // 2 * 2:2]
    margin = jnp.minimum(tallies[source_of] - 1, most - tallies[receiver]) // 2
    margin = jnp.where((source_of == order[0]) | (receiver == order[0]) | (tallies[receiver] == 0), 0, jnp.maximum(margin, 0))
    shifted = jax.random.randint(jax.random.fold_in(own, 4), (amount // 2,), 0, 1 << 20) % (margin + 1)
    tallies = tallies.at[source_of].add(-shifted).at[receiver].add(shifted)
    labels = jnp.searchsorted(jnp.cumsum(tallies), jnp.arange(rows * top), side="right").astype(jnp.int32)
    table = labels.reshape(top, rows).T
    table = table[jax.random.permutation(jax.random.fold_in(own, 1), rows)]
    turn = jax.random.randint(jax.random.fold_in(own, 2), (rows, 1), 0, top)
    return jnp.take_along_axis(table, (jnp.arange(top)[None, :] + turn) % top, axis=1)


def portions_of(number_of, total, bound, slope, full):
    portions = [(1 << 20) // math.isqrt(rank ** slope) + 1 for rank in range(1, number_of + 1)]
    largest = bound if full else min(bound, max(-(-total // number_of), total * portions[0] // sum(portions)))
    least = 1 if total - largest >= number_of - 1 else 0
    holding, rest = [largest] + [least] * (number_of - 1), total - largest - least * (number_of - 1)
    while rest > 0:
        free = [i for i in range(1, number_of) if holding[i] < largest] or [i for i in range(1, number_of) if holding[i] < bound]
        pool, left = sum([portions[i] for i in free]), rest
        for i in free:
            addition = min(bound - holding[i], max(1, left * portions[i] // pool), rest)
            holding[i] = holding[i] + addition
            rest = rest - addition
    return np.array(holding)


def centred(rng, shape, scale, reach, shards=(), kind=jnp.bfloat16):
    values = jax.random.normal(rng, shape, jnp.float32) * scale
    if len(shards) > 0:
        values = block_levels(rng, shape, shards, -0.22, 0.18) * values
    return jnp.clip(values, min=-reach, max=reach).astype(kind)


def setup_inputs(seed: int = 0) -> dict:
    arg_keys = jax.random.split(jax.random.key(seed), 11)
    forward_state = centred(arg_keys[0], (SECTIONS, TOKENS, D), 1.0, 6.0, ((0, 8), (1, 64)))
    grad_state = centred(arg_keys[1], (SECTIONS, TOKENS, D), 1.0, 6.0, ((0, 8), (1, 64)))
    forward_routes_keys = jax.random.split(jax.random.fold_in(arg_keys[2], 1), SECTIONS * TOKENS // TOK_DEV)
    forward_routes_turns = jax.random.permutation(jax.random.fold_in(arg_keys[2], 3), SECTIONS * TOKENS // TOK_DEV)
    forward_routes = jax.vmap(lambda own, number: assign_block(jax.random.fold_in(arg_keys[2], 2), own, number, TOK_DEV, EXPERTS, TOP, CAP, 0))(forward_routes_keys, forward_routes_turns).reshape((SECTIONS, TOKENS, TOP))
    forward_gates = jnp.clip(jnp.exp(math.log(2.0) - 2.306499 * jax.random.uniform(arg_keys[3], (SECTIONS, TOKENS, TOP), jnp.float32) ** block_levels(arg_keys[3], (SECTIONS, TOKENS, TOP), ((0, 8), (1, 64)), -0.2, 0.2)), 0.19921875, 2.0).astype(jnp.bfloat16)
    backward_routes_keys = jax.random.split(jax.random.fold_in(arg_keys[4], 1), SECTIONS * TOKENS // TOK_DEV)
    backward_routes_turns = jax.random.permutation(jax.random.fold_in(arg_keys[4], 3), SECTIONS * TOKENS // TOK_DEV)
    backward_routes = jax.vmap(lambda own, number: assign_block(jax.random.fold_in(arg_keys[4], 2), own, number, TOK_DEV, EXPERTS, TOP, CAP, 0))(backward_routes_keys, backward_routes_turns).reshape((SECTIONS, TOKENS, TOP))
    backward_gates = jnp.clip(jnp.exp(math.log(2.0) - 2.306499 * jax.random.uniform(arg_keys[5], (SECTIONS, TOKENS, TOP), jnp.float32) ** block_levels(arg_keys[5], (SECTIONS, TOKENS, TOP), ((0, 8), (1, 64)), -0.2, 0.2)), 0.19921875, 2.0).astype(jnp.bfloat16)
    saved_preacts = centred(arg_keys[6], (SECTIONS, 2, SOURCES, CAP, EXPERTS * FF), 1.5, 6.0, ((0, 8), (4, 64)))
    gate_weight = centred(arg_keys[7], (SECTIONS, D, EXPERTS * FF), D ** -0.5, 0.09375, ((0, 8), (2, 64)))
    up_weight = centred(arg_keys[8], (SECTIONS, D, EXPERTS * FF), D ** -0.5, 0.09375, ((0, 8), (2, 64)))
    down_weight = centred(arg_keys[9], (SECTIONS, EXPERTS * FF, D), FF ** -0.5, 0.1875, ((0, 8), (1, 64)))
    return dict(forward_state=forward_state, grad_state=grad_state, forward_routes=forward_routes, forward_gates=forward_gates, backward_routes=backward_routes, backward_gates=backward_gates, saved_preacts=saved_preacts, gate_weight=gate_weight, up_weight=up_weight, down_weight=down_weight)


def slot_tables(routes, gate_values, expert_count, capacity):
    tokens_here, picked = routes.shape
    expert_ids = jnp.arange(expert_count, dtype=jnp.int32)
    chosen = (routes[:, :, None] == expert_ids).astype(jnp.int32)
    flat_hits = chosen.reshape(tokens_here * picked, expert_count)
    earlier = jnp.cumsum(flat_hits, axis=0) - flat_hits
    position = jnp.sum(earlier * flat_hits, axis=1).reshape(tokens_here, picked)
    slot_ids = jnp.arange(capacity, dtype=jnp.int32)
    placed = chosen[:, :, :, None] * (position[:, :, None, None] == slot_ids).astype(jnp.int32)
    table = jnp.transpose(jnp.sum(placed, axis=1), (1, 2, 0)).astype(jnp.float32)
    scaled = placed.astype(jnp.float32) * gate_values.astype(jnp.float32)[:, :, None, None]
    weighted = jnp.transpose(jnp.sum(scaled, axis=1), (1, 2, 0))
    return table, weighted


def group_tables(routes, gate_values):
    maker = jax.vmap(partial(slot_tables, expert_count=EXPERTS, capacity=CAP))
    return maker(routes.reshape(SOURCES, TOK_DEV, TOP), gate_values.reshape(SOURCES, TOK_DEV, TOP))


def sum_blocks(pieces):
    rounded = lax.optimization_barrier(pieces.astype(jnp.bfloat16))
    return jnp.sum(rounded.astype(jnp.float32), axis=1)


def section_forward(activations, routes, gate_values, gate_weight, up_weight, down_weight):
    table, weighted = group_tables(routes, gate_values)
    grouped = activations.reshape(SOURCES, TOK_DEV, D).astype(jnp.float32)
    slot_rows = jnp.einsum("sect,std->escd", table, grouped).astype(jnp.bfloat16)
    count = SOURCES * CAP
    outputs = []
    for expert in range(EXPERTS):
        start = expert * FF
        block_rows = slot_rows[expert].reshape(count, D)
        pre_gate = jnp.dot(block_rows, gate_weight[:, start:start + FF], preferred_element_type=jnp.float32)
        pre_up = jnp.dot(block_rows, up_weight[:, start:start + FF], preferred_element_type=jnp.float32)
        hidden = (jax.nn.silu(pre_gate) * pre_up).astype(jnp.bfloat16)
        pieces = jnp.einsum("nsf,sfd->nsd", hidden.reshape(count, WSPLIT, FF_DEV).astype(jnp.float32),
                            down_weight[start:start + FF].reshape(WSPLIT, FF_DEV, D).astype(jnp.float32))
        outputs.append(sum_blocks(pieces).reshape(SOURCES, CAP, D))
    combined = jnp.stack(outputs)
    mixed = grouped + jnp.einsum("sect,escd->std", weighted, combined)
    return mixed.reshape(TOKENS, D).astype(jnp.bfloat16)


def section_backward(cotangent, routes, gate_values, saved, gate_weight, up_weight, down_weight):
    table, weighted = group_tables(routes, gate_values)
    grouped = cotangent.reshape(SOURCES, TOK_DEV, D).astype(jnp.float32)
    scaled = jnp.einsum("sect,std->escd", weighted, grouped).astype(jnp.bfloat16)
    count = SOURCES * CAP
    outputs = []
    for expert in range(EXPERTS):
        start = expert * FF
        block_rows = scaled[expert].reshape(count, D)
        hidden_grad = jnp.dot(block_rows, down_weight[start:start + FF].T, preferred_element_type=jnp.float32)
        pre_gate = saved[0, :, :, start:start + FF].reshape(count, FF).astype(jnp.float32)
        pre_up = saved[1, :, :, start:start + FF].reshape(count, FF).astype(jnp.float32)
        sig = jax.nn.sigmoid(pre_gate)
        grad_gate = (hidden_grad * pre_up * sig * (1.0 + pre_gate * (1.0 - sig))).astype(jnp.bfloat16)
        grad_up = (hidden_grad * pre_gate * sig).astype(jnp.bfloat16)
        gate_part = jnp.einsum("nsf,dsf->nsd", grad_gate.reshape(count, WSPLIT, FF_DEV).astype(jnp.float32),
                               gate_weight[:, start:start + FF].reshape(D, WSPLIT, FF_DEV).astype(jnp.float32))
        up_part = jnp.einsum("nsf,dsf->nsd", grad_up.reshape(count, WSPLIT, FF_DEV).astype(jnp.float32),
                             up_weight[:, start:start + FF].reshape(D, WSPLIT, FF_DEV).astype(jnp.float32))
        outputs.append(sum_blocks(gate_part + up_part).reshape(SOURCES, CAP, D))
    combined = jnp.stack(outputs)
    result = grouped + jnp.einsum("sect,escd->std", table, combined)
    return result.reshape(TOKENS, D).astype(jnp.bfloat16)


def reference(forward_state, grad_state, forward_routes, forward_gates, backward_routes, backward_gates,
              saved_preacts, gate_weight, up_weight, down_weight):
    results = [section_forward(forward_state[section], forward_routes[section], forward_gates[section],
                             gate_weight[section], up_weight[section], down_weight[section]) for section in range(SECTIONS)]
    gradients = [section_backward(grad_state[section], backward_routes[section], backward_gates[section],
                                saved_preacts[section], gate_weight[section], up_weight[section],
                                down_weight[section]) for section in range(SECTIONS)]
    forward_next = jnp.stack([results[(section - 1) % SECTIONS] for section in range(SECTIONS)])
    backward_next = jnp.stack([gradients[(section + 1) % SECTIONS] for section in range(SECTIONS)])
    return forward_next, backward_next
```

```python
import jax
import jax.numpy as jnp
from jax import lax
from jax.sharding import Mesh, PartitionSpec as P

BF = jnp.bfloat16
F32 = jnp.float32
ROWS_T = (((1,), (1,)), ((), ()))


def shift(block, axis, distance):
    n = lax.axis_size(axis)
    return lax.ppermute(block, axis, [(i, (i + distance) % n) for i in range(n)])


def exchange(block):
    return lax.all_to_all(block, "z", split_axis=0, concat_axis=0, tiled=True)


def slot_tables(routes, gate_values, expert_count, capacity):
    tokens_here, picked = routes.shape
    expert_ids = jnp.arange(expert_count, dtype=jnp.int32)
    chosen = (routes[:, :, None] == expert_ids).astype(jnp.int32)
    flat_hits = chosen.reshape(tokens_here * picked, expert_count)
    earlier = jnp.cumsum(flat_hits, axis=0) - flat_hits
    position = jnp.sum(earlier * flat_hits, axis=1).reshape(tokens_here, picked)
    slot_ids = jnp.arange(capacity, dtype=jnp.int32)
    placed = chosen[:, :, :, None] * (position[:, :, None, None] == slot_ids).astype(jnp.int32)
    table = jnp.transpose(jnp.sum(placed, axis=1), (1, 2, 0)).astype(BF)
    scaled = placed.astype(BF) * gate_values[:, :, None, None]
    weighted = jnp.transpose(jnp.sum(scaled, axis=1), (1, 2, 0)).astype(BF)
    slots = expert_count * capacity
    return table.reshape(slots, tokens_here), weighted.reshape(slots, tokens_here)


def pack(table, rows):
    return jnp.dot(table, rows, preferred_element_type=F32).astype(BF)


def merge(returned, table, base):
    combined = lax.dot_general(
        table, returned, (((0,), (0,)), ((), ())), preferred_element_type=F32
    )
    return (base.astype(F32) + combined).astype(BF)


def forward_block(rows, gates, ups, downs):
    total = None
    for gate, up, down in zip(gates, ups, downs):
        pre_gate = jnp.dot(rows, gate, preferred_element_type=F32)
        pre_up = jnp.dot(rows, up, preferred_element_type=F32)
        hidden = (jax.nn.silu(pre_gate) * pre_up).astype(BF)
        piece = jnp.dot(hidden, down, preferred_element_type=F32)
        total = piece if total is None else total + piece
    return total


def backward_block(rows, saved, gates, ups, downs):
    total = None
    for kept, gate, up, down in zip(saved, gates, ups, downs):
        hidden_grad = lax.dot_general(rows, down, ROWS_T, preferred_element_type=F32)
        a, b = kept[0].astype(F32), kept[1].astype(F32)
        sig = jax.nn.sigmoid(a)
        grad_gate = (hidden_grad * b * sig * (1.0 + a * (1.0 - sig))).astype(BF)
        grad_up = (hidden_grad * a * sig).astype(BF)
        piece = lax.dot_general(grad_gate, gate, ROWS_T, preferred_element_type=F32)
        piece = piece + lax.dot_general(grad_up, up, ROWS_T, preferred_element_type=F32)
        total = piece if total is None else total + piece
    return total


def spread_and_sum(rows, compute):
    n = lax.axis_size("x")
    total = compute(rows, 0)
    for k in range(1, n):
        visiting = shift(rows, "x", -k)
        total = total + shift(compute(visiting, k).astype(BF), "x", k).astype(F32)
    return total.astype(BF)


def body(
    forward_state, grad_state, forward_routes, forward_gates, backward_routes, backward_gates,
    saved_preacts, gate_weight, up_weight, down_weight,
):
    x, y, saved = forward_state[0], grad_state[0], saved_preacts[0]
    width = x.shape[1]
    capacity, units = saved.shape[2], saved.shape[3]
    nz, nx, nc = lax.axis_size("z"), lax.axis_size("x"), lax.axis_size("c")
    f_table, f_weighted = slot_tables(forward_routes[0], forward_gates[0], nz, capacity)
    b_table, b_weighted = slot_tables(backward_routes[0], backward_gates[0], nz, capacity)
    f_rows = exchange(pack(f_table, x).reshape(nz, capacity, width)).reshape(-1, width)
    b_rows = exchange(pack(b_weighted, y).reshape(nz, capacity, width)).reshape(-1, width)

    gates = (gate_weight[0], shift(gate_weight[0], "c", 1))
    ups = (up_weight[0], shift(up_weight[0], "c", 1))
    downs = (down_weight[0], shift(down_weight[0], "c", 1))
    me_x, me_c = lax.axis_index("x"), lax.axis_index("c")
    by_core = saved.reshape(2, nz, nx, nc, capacity, units)
    mine = lax.dynamic_index_in_dim(by_core, me_c, 3, keepdims=False)
    theirs = shift(lax.dynamic_index_in_dim(by_core, 1 - me_c, 3, keepdims=False), "c", 1)

    def saved_of(k):
        at = lax.rem(me_x + k, nx)
        return tuple(
            lax.dynamic_index_in_dim(kept, at, 2, keepdims=False).reshape(2, nz * capacity, units)
            for kept in (mine, theirs)
        )

    f_out = spread_and_sum(f_rows, lambda rows, k: forward_block(rows, gates, ups, downs))
    b_out = spread_and_sum(
        b_rows, lambda rows, k: backward_block(rows, saved_of(k), gates, ups, downs)
    )
    f_back = exchange(f_out.reshape(nz, capacity, width)).reshape(-1, width)
    b_back = exchange(b_out.reshape(nz, capacity, width)).reshape(-1, width)
    result = merge(f_back, f_weighted, x)
    gradient = merge(b_back, b_table, y)
    ring = lax.axis_size(("h", "y"))
    forward_next = lax.ppermute(result, ("h", "y"), [(i, (i + 1) % ring) for i in range(ring)])
    backward_next = lax.ppermute(gradient, ("h", "y"), [(i, (i - 1) % ring) for i in range(ring)])
    return forward_next[None], backward_next[None]


def solution(mesh):
    pipes = mesh.shape["pipe"]
    fine = Mesh(mesh.devices.reshape(2, pipes // 2, 8, 4, 2), ("h", "y", "z", "x", "c"))
    pipe, expert = ("h", "y"), ("z", "x", "c")
    tokens = P(pipe, expert, None)
    return jax.shard_map(
        body,
        mesh=fine,
        in_specs=(
            tokens, tokens, tokens, tokens, tokens, tokens,
            P(pipe, None, None, None, expert),
            P(pipe, None, expert),
            P(pipe, None, expert),
            P(pipe, expert, None),
        ),
        out_specs=(tokens, tokens),
        check_vma=False,
    )
```

```python
import functools

import jax
import jax.numpy as jnp
from jax import lax
from jax.experimental import pallas as pl
from jax.experimental.pallas import tpu as pltpu
from jax.sharding import Mesh, PartitionSpec as P

BF = jnp.bfloat16
F32 = jnp.float32
ROWS_T = (((1,), (1,)), ((), ()))
COLUMNS = 512


def permute(block, axis, targets):
    return lax.ppermute(block, axis, list(enumerate(targets)))


def swap_core(block):
    return permute(block, "c", (1, 0))


def swap_weights_x(block):
    return permute(block, "x", (1, 0, 3, 2))


def swap_rows_x(block):
    return permute(block, "x", (3, 2, 1, 0))


def exchange(block):
    return lax.all_to_all(block, "z", split_axis=0, concat_axis=0, tiled=True)


def slot_tables(routes, gate_values, expert_count, capacity):
    tokens_here, picked = routes.shape
    expert_ids = jnp.arange(expert_count, dtype=jnp.int32)
    chosen = (routes[:, :, None] == expert_ids).astype(jnp.int32)
    flat_hits = chosen.reshape(tokens_here * picked, expert_count)
    earlier = jnp.cumsum(flat_hits, axis=0) - flat_hits
    position = jnp.sum(earlier * flat_hits, axis=1).reshape(tokens_here, picked)
    slot_ids = jnp.arange(capacity, dtype=jnp.int32)
    placed = chosen[:, :, :, None] * (position[:, :, None, None] == slot_ids).astype(jnp.int32)
    table = jnp.transpose(jnp.sum(placed, axis=1), (1, 2, 0)).astype(BF)
    scaled = placed.astype(BF) * gate_values[:, :, None, None]
    weighted = jnp.transpose(jnp.sum(scaled, axis=1), (1, 2, 0)).astype(BF)
    slots = expert_count * capacity
    return table.reshape(slots, tokens_here), weighted.reshape(slots, tokens_here)


def pack(table, rows):
    return jnp.dot(table, rows, preferred_element_type=F32).astype(BF)


def merge(returned, table, base):
    combined = lax.dot_general(
        table, returned, (((0,), (0,)), ((), ())), preferred_element_type=F32
    )
    return (base.astype(F32) + combined).astype(BF)


def load_weights(refs, gate_up, down, sems):
    units = down.shape[1]
    copies = []
    for u in range(4):
        copies.append(pltpu.make_async_copy(refs[u], gate_up.at[u, :, pl.ds(0, units)], sems.at[u]))
        copies.append(
            pltpu.make_async_copy(refs[4 + u], gate_up.at[u, :, pl.ds(units, units)], sems.at[4 + u])
        )
        copies.append(pltpu.make_async_copy(refs[8 + u], down.at[u], sems.at[8 + u]))
    return copies


def forward_kernel(own, visiting, *refs):
    weights, (out_own, out_visiting, rows, gate_up, down, hidden, sems) = refs[:12], refs[12:]
    copies = load_weights(weights, gate_up, down, sems)
    for copy in copies:
        copy.start()
    half, width = own.shape
    units = down.shape[1]
    rows[pl.ds(0, half), :] = own[...]
    rows[pl.ds(half, half), :] = visiting[...]
    for u in range(4):
        copies[3 * u].wait()
        copies[3 * u + 1].wait()
        pre = jnp.dot(rows[...], gate_up[u], preferred_element_type=F32)
        gate, up = pre[:, :units], pre[:, units:]
        hidden[u] = (gate * jax.nn.sigmoid(gate) * up).astype(BF)
    for u in range(4):
        copies[3 * u + 2].wait()
    for start in range(0, width, COLUMNS):
        at = pl.ds(start, COLUMNS)
        total = jnp.dot(hidden[0], down[0, :, at], preferred_element_type=F32)
        for u in range(1, 4):
            total = total + jnp.dot(hidden[u], down[u, :, at], preferred_element_type=F32)
        out_own[:, at] = total[:half]
        out_visiting[:, at] = total[half:].astype(BF)


def backward_kernel(own, visiting, saved, *refs):
    weights, (out_own, out_visiting, rows, gate_up, down, grads, sems) = refs[:12], refs[12:]
    copies = load_weights(weights, gate_up, down, sems)
    for copy in copies:
        copy.start()
    half, width = own.shape
    units = down.shape[1]
    rows[pl.ds(0, half), :] = own[...]
    rows[pl.ds(half, half), :] = visiting[...]
    for u in range(4):
        copies[3 * u + 2].wait()
        grad = lax.dot_general(rows[...], down[u], ROWS_T, preferred_element_type=F32)
        a, b = saved[u, 0].astype(F32), saved[u, 1].astype(F32)
        sig = jax.nn.sigmoid(a)
        grads[u, :, pl.ds(0, units)] = (grad * b * sig * (1.0 + a * (1.0 - sig))).astype(BF)
        grads[u, :, pl.ds(units, units)] = (grad * a * sig).astype(BF)
    for u in range(4):
        copies[3 * u].wait()
        copies[3 * u + 1].wait()
    for start in range(0, width, COLUMNS):
        at = pl.ds(start, COLUMNS)
        total = lax.dot_general(grads[0], gate_up[0, at, :], ROWS_T, preferred_element_type=F32)
        for u in range(1, 4):
            total = total + lax.dot_general(
                grads[u], gate_up[u, at, :], ROWS_T, preferred_element_type=F32
            )
        out_own[:, at] = total[:half]
        out_visiting[:, at] = total[half:].astype(BF)


def expert_pass(kernel, own, visiting, extra, weights, middle):
    half, width = own.shape
    units = weights[8].shape[0]
    vmem = pl.BlockSpec(memory_space=pltpu.VMEM)
    rows, flops = 2 * half, 2 * 2 * half * width * 4 * units * 3
    return pl.pallas_call(
        kernel,
        out_shape=(
            jax.ShapeDtypeStruct((half, width), F32),
            jax.ShapeDtypeStruct((half, width), BF),
        ),
        in_specs=[vmem] * (2 + len(extra)) + [pl.BlockSpec(memory_space=pl.ANY)] * 12,
        out_specs=(vmem, vmem),
        scratch_shapes=[
            pltpu.VMEM((rows, width), BF),
            pltpu.VMEM((4, width, 2 * units), BF),
            pltpu.VMEM((4, units, width), BF),
            pltpu.VMEM((4, rows, middle), BF),
            pltpu.SemaphoreType.DMA((12,)),
        ],
        compiler_params=pltpu.CompilerParams(vmem_limit_bytes=40 * 1024 * 1024),
        cost_estimate=pl.CostEstimate(
            flops=flops, bytes_accessed=12 * width * units * 2 + 5 * half * width * 2, transcendentals=0
        ),
    )(own, visiting, *extra, *weights)


def body(
    forward_state, grad_state, forward_routes, forward_gates, backward_routes, backward_gates,
    saved_preacts, gate_weight, up_weight, down_weight,
):
    x, y, saved = forward_state[0], grad_state[0], saved_preacts[0]
    width = x.shape[1]
    capacity, units = saved.shape[2], saved.shape[3]
    nz, nx, nc = lax.axis_size("z"), lax.axis_size("x"), lax.axis_size("c")
    f_table, f_weighted = slot_tables(forward_routes[0], forward_gates[0], nz, capacity)
    b_table, b_weighted = slot_tables(backward_routes[0], backward_gates[0], nz, capacity)
    f_rows = exchange(pack(f_table, x).reshape(nz, capacity, width)).reshape(-1, width)
    b_rows = exchange(pack(b_weighted, y).reshape(nz, capacity, width)).reshape(-1, width)

    own_weights = (gate_weight[0], up_weight[0], down_weight[0])
    beside_weights = [swap_weights_x(mine) for mine in own_weights]
    f_visiting = swap_rows_x(f_rows)
    f_visiting, *beside_weights = lax.optimization_barrier((f_visiting, *beside_weights))
    weights = []
    for mine, beside in zip(own_weights, beside_weights):
        weights += [mine, swap_core(mine), beside, swap_core(beside)]

    me_x, me_c = lax.axis_index("x"), lax.axis_index("c")
    by_place = saved.reshape(2, nz, nx, nc, capacity, units)

    def kept_for(at_x):
        rows_of = [
            lax.dynamic_index_in_dim(by_place, at, 2, keepdims=False) for at in (at_x, nx - 1 - at_x)
        ]
        return jnp.stack(rows_of, 1)

    here = jnp.stack([kept_for(me_x), swap_weights_x(kept_for(me_x ^ 1))])
    mine = lax.dynamic_index_in_dim(here, me_c, 4, keepdims=False)
    theirs = swap_core(lax.dynamic_index_in_dim(here, 1 - me_c, 4, keepdims=False))
    kept = jnp.stack([mine, theirs], 1).reshape(4, 2, 2 * nz * capacity, units)

    f_own, f_visited = expert_pass(
        forward_kernel, f_rows, f_visiting, (), weights, units
    )
    b_own, b_visited = expert_pass(
        backward_kernel, b_rows, swap_rows_x(b_rows), (kept,), weights, 2 * units
    )
    f_out = (f_own + swap_rows_x(f_visited).astype(F32)).astype(BF)
    b_out = (b_own + swap_rows_x(b_visited).astype(F32)).astype(BF)
    f_back = exchange(f_out.reshape(nz, capacity, width)).reshape(-1, width)
    b_back = exchange(b_out.reshape(nz, capacity, width)).reshape(-1, width)
    result = merge(f_back, f_weighted, x)
    gradient = merge(b_back, b_table, y)
    ring = lax.axis_size(("h", "y"))
    forward_next = permute(result, ("h", "y"), [(i + 1) % ring for i in range(ring)])
    backward_next = permute(gradient, ("h", "y"), [(i - 1) % ring for i in range(ring)])
    return forward_next[None], backward_next[None]


def solution(mesh):
    pipes = mesh.shape["pipe"]
    fine = Mesh(mesh.devices.reshape(2, pipes // 2, 8, 4, 2), ("h", "y", "z", "x", "c"))
    pipe, expert = ("h", "y"), ("z", "x", "c")
    tokens = P(pipe, expert, None)
    return jax.shard_map(
        body,
        mesh=fine,
        in_specs=(
            tokens, tokens, tokens, tokens, tokens, tokens,
            P(pipe, None, None, None, expert),
            P(pipe, None, expert),
            P(pipe, None, expert),
            P(pipe, expert, None),
        ),
        out_specs=(tokens, tokens),
        check_vma=False,
    )
```

```python
import jax
import jax.numpy as jnp
from jax import lax
from jax.experimental import pallas as pl
from jax.experimental.pallas import tpu as pltpu
from jax.sharding import Mesh, PartitionSpec as P

BF = jnp.bfloat16
F32 = jnp.float32
ROWS_T = (((1,), (1,)), ((), ()))
COLUMNS = 512
GATE_COLUMNS = 128
VMEM = pl.BlockSpec(memory_space=pltpu.VMEM)


def permute(block, axis, targets):
    return lax.ppermute(block, axis, list(enumerate(targets)))


def swap_core(block):
    return permute(block, "c", (1, 0))


def swap_weights_x(block):
    return permute(block, "x", (1, 0, 3, 2))


def swap_rows_x(block):
    return permute(block, "x", (3, 2, 1, 0))


def exchange(block):
    return lax.all_to_all(block, "z", split_axis=0, concat_axis=0, tiled=True)


def pair_mask(r_col, r_row, passes):
    rows = jax.lax.broadcasted_iota(jnp.int32, (r_col.shape[0], r_row.shape[1]), 0)
    cols = jax.lax.broadcasted_iota(jnp.int32, (r_col.shape[0], r_row.shape[1]), 1)
    same = r_col == r_row
    if passes > 1:
        per_pass = r_row.shape[1] // passes
        same = same & ((rows >= per_pass) == (cols >= per_pass))
    return same, rows, cols


def pack_kernel(r_row, r_col, gate_col, x, y, out):
    tokens, width = x.shape
    same, rows, cols = pair_mask(r_col[...], r_row[...], 2)
    slot = jnp.sum((same & (rows < cols)).astype(jnp.int32), axis=0, keepdims=True)
    second = (cols[:1] >= tokens).astype(jnp.int32)
    key = r_row[...] * 16 + second * 8 + slot
    table = (rows == key).astype(F32).astype(BF)
    for start in range(0, width, COLUMNS):
        at = pl.ds(start, COLUMNS)
        picked = jnp.dot(table[:, :tokens], x[:, at], preferred_element_type=F32)
        picked = picked + jnp.dot(table[:, tokens:], y[:, at], preferred_element_type=F32)
        out[:, at] = picked.astype(BF)
    gates = jnp.broadcast_to(gate_col[...], (2 * tokens, GATE_COLUMNS)).astype(BF)
    out[:, pl.ds(width, GATE_COLUMNS)] = jnp.dot(
        table, gates, preferred_element_type=F32
    ).astype(BF)


def pack(f_routes, b_routes, f_gates, b_gates, x, y):
    tokens, width = x.shape
    routes = jnp.concatenate([f_routes, b_routes])
    gates = jnp.concatenate([f_gates, b_gates]).astype(F32)
    return pl.pallas_call(
        pack_kernel,
        out_shape=jax.ShapeDtypeStruct((2 * tokens, width + GATE_COLUMNS), BF),
        in_specs=[VMEM] * 5,
        out_specs=VMEM,
        cost_estimate=pl.CostEstimate(
            flops=8 * tokens * tokens * width, bytes_accessed=8 * tokens * width, transcendentals=0
        ),
    )(routes.reshape(1, -1), routes, gates, x, y)


def unpack_kernel(r_row, r_col, slots, out):
    width = slots.shape[1]
    same, rows, cols = pair_mask(r_col[...], r_row[...], 1)
    slot = jnp.sum((same & (cols < rows)).astype(jnp.int32), axis=1, keepdims=True)
    table = (cols == r_col[...] * 8 + slot).astype(F32).astype(BF)
    for start in range(0, width, COLUMNS):
        at = pl.ds(start, COLUMNS)
        out[:, at] = jnp.dot(table, slots[:, at], preferred_element_type=F32).astype(BF)


def unpack(routes, slots):
    tokens, width = slots.shape
    return pl.pallas_call(
        unpack_kernel,
        out_shape=jax.ShapeDtypeStruct((tokens, width), BF),
        in_specs=[VMEM] * 3,
        out_specs=VMEM,
        cost_estimate=pl.CostEstimate(
            flops=2 * tokens * tokens * width, bytes_accessed=4 * tokens * width, transcendentals=0
        ),
    )(routes.reshape(1, -1), routes, slots)


def to_section(block, step):
    last, first, beside = (3, 0, 2) if step == 1 else (0, 3, 1)
    half = block.shape[0] // 2
    pairs = [(i, (i + step) % 8) for i in range(8)]
    axes = ("h", "y")
    straight = lax.ppermute(block[:half], axes, pairs)
    inside = lax.ppermute(block[half:], axes, [(a, b) for a, b in pairs if a // 4 == b // 4])
    away = lax.ppermute(block[half:], axes, [(4 * h + last, 4 * h + beside) for h in (0, 1)])
    across = lax.ppermute(away, axes, [(4 * h + beside, 4 * (1 - h) + first) for h in (0, 1)])
    rest = jnp.where(lax.axis_index("y") == first, across, inside)
    return jnp.concatenate([straight, rest])


def load_weights(refs, gate_up, down, sems):
    units = down.shape[1]
    copies = []
    for u in range(4):
        copies.append(pltpu.make_async_copy(refs[u], gate_up.at[u, :, pl.ds(0, units)], sems.at[u]))
        copies.append(
            pltpu.make_async_copy(refs[4 + u], gate_up.at[u, :, pl.ds(units, units)], sems.at[4 + u])
        )
        copies.append(pltpu.make_async_copy(refs[8 + u], down.at[u], sems.at[8 + u]))
    return copies


def forward_kernel(own, visiting, *refs):
    weights, (out_own, out_visiting, rows, gate_up, down, hidden, sems) = refs[:12], refs[12:]
    copies = load_weights(weights, gate_up, down, sems)
    for copy in copies:
        copy.start()
    half, width = out_own.shape
    units = down.shape[1]
    gates = [ref[:, pl.ds(width, GATE_COLUMNS)].astype(F32)[:, :1] for ref in (own, visiting)]
    rows[pl.ds(0, half), :] = own[:, pl.ds(0, width)]
    rows[pl.ds(half, half), :] = visiting[:, pl.ds(0, width)]
    for u in range(4):
        copies[3 * u].wait()
        copies[3 * u + 1].wait()
        pre = jnp.dot(rows[...], gate_up[u], preferred_element_type=F32)
        gate, up = pre[:, :units], pre[:, units:]
        hidden[u] = (gate * jax.nn.sigmoid(gate) * up).astype(BF)
    for u in range(4):
        copies[3 * u + 2].wait()
    for start in range(0, width, COLUMNS):
        at = pl.ds(start, COLUMNS)
        total = jnp.dot(hidden[0], down[0, :, at], preferred_element_type=F32)
        for u in range(1, 4):
            total = total + jnp.dot(hidden[u], down[u, :, at], preferred_element_type=F32)
        out_own[:, at] = own[:, at].astype(F32) + gates[0] * total[:half]
        out_visiting[:, at] = (gates[1] * total[half:]).astype(BF)


def backward_kernel(own, visiting, saved, *refs):
    weights, (out_own, out_visiting, rows, gate_up, down, grads, sems) = refs[:12], refs[12:]
    copies = load_weights(weights, gate_up, down, sems)
    for copy in copies:
        copy.start()
    half, width = out_own.shape
    units = down.shape[1]
    for at_row, ref in ((0, own), (half, visiting)):
        gate = ref[:, pl.ds(width, GATE_COLUMNS)].astype(F32)[:, :1]
        for start in range(0, width, COLUMNS):
            at = pl.ds(start, COLUMNS)
            rows[pl.ds(at_row, half), at] = (gate * ref[:, at].astype(F32)).astype(BF)
    for u in range(4):
        copies[3 * u + 2].wait()
        grad = lax.dot_general(rows[...], down[u], ROWS_T, preferred_element_type=F32)
        a, b = saved[u, 0].astype(F32), saved[u, 1].astype(F32)
        sig = jax.nn.sigmoid(a)
        grads[u, :, pl.ds(0, units)] = (grad * b * sig * (1.0 + a * (1.0 - sig))).astype(BF)
        grads[u, :, pl.ds(units, units)] = (grad * a * sig).astype(BF)
    for u in range(4):
        copies[3 * u].wait()
        copies[3 * u + 1].wait()
    for start in range(0, width, COLUMNS):
        at = pl.ds(start, COLUMNS)
        total = lax.dot_general(grads[0], gate_up[0, at, :], ROWS_T, preferred_element_type=F32)
        for u in range(1, 4):
            total = total + lax.dot_general(
                grads[u], gate_up[u, at, :], ROWS_T, preferred_element_type=F32
            )
        out_own[:, at] = own[:, at].astype(F32) + total[:half]
        out_visiting[:, at] = total[half:].astype(BF)


def expert_pass(kernel, own, visiting, extra, weights, middle):
    half, units = own.shape[0], weights[8].shape[0]
    width = own.shape[1] - GATE_COLUMNS
    rows, flops = 2 * half, 2 * 2 * half * width * 4 * units * 3
    return pl.pallas_call(
        kernel,
        out_shape=(
            jax.ShapeDtypeStruct((half, width), F32),
            jax.ShapeDtypeStruct((half, width), BF),
        ),
        in_specs=[VMEM] * (2 + len(extra)) + [pl.BlockSpec(memory_space=pl.ANY)] * 12,
        out_specs=(VMEM, VMEM),
        scratch_shapes=[
            pltpu.VMEM((rows, width), BF),
            pltpu.VMEM((4, width, 2 * units), BF),
            pltpu.VMEM((4, units, width), BF),
            pltpu.VMEM((4, rows, middle), BF),
            pltpu.SemaphoreType.DMA((12,)),
        ],
        compiler_params=pltpu.CompilerParams(vmem_limit_bytes=40 * 1024 * 1024),
        cost_estimate=pl.CostEstimate(
            flops=flops, bytes_accessed=12 * width * units * 2 + 5 * half * width * 2, transcendentals=0
        ),
    )(own, visiting, *extra, *weights)


def body(
    forward_state, grad_state, forward_routes, forward_gates, backward_routes, backward_gates,
    saved_preacts, gate_weight, up_weight, down_weight,
):
    x, y, saved = forward_state[0], grad_state[0], saved_preacts[0]
    width = x.shape[1]
    capacity, units = saved.shape[2], saved.shape[3]
    nz, nx, nc = lax.axis_size("z"), lax.axis_size("x"), lax.axis_size("c")
    packed = pack(
        forward_routes[0], backward_routes[0], forward_gates[0], backward_gates[0], x, y
    )
    arrived = exchange(packed.reshape(nz, 2 * capacity, packed.shape[1]))
    f_rows = arrived[:, :capacity].reshape(nz * capacity, -1)
    b_rows = arrived[:, capacity:].reshape(nz * capacity, -1)
    f_visiting, b_visiting = swap_rows_x(f_rows), swap_rows_x(b_rows)

    me_x, me_c = lax.axis_index("x"), lax.axis_index("c")
    by_place = saved.reshape(2, nz, nx, nc, capacity, units)

    def kept_for(at_x):
        rows_of = [
            lax.dynamic_index_in_dim(by_place, at, 2, keepdims=False) for at in (at_x, nx - 1 - at_x)
        ]
        return jnp.stack(rows_of, 1)

    here = jnp.stack([kept_for(me_x), swap_weights_x(kept_for(me_x ^ 1))])
    mine = lax.dynamic_index_in_dim(here, me_c, 4, keepdims=False)
    theirs = swap_core(lax.dynamic_index_in_dim(here, 1 - me_c, 4, keepdims=False))
    kept = jnp.stack([mine, theirs], 1).reshape(4, 2, 2 * nz * capacity, units)

    own_weights = (gate_weight[0], up_weight[0], down_weight[0])
    beside_weights = [swap_weights_x(mine) for mine in own_weights]
    f_visiting, beside_weights[2], kept = lax.optimization_barrier(
        (f_visiting, beside_weights[2], kept)
    )
    weights = []
    for mine, beside in zip(own_weights, beside_weights):
        weights += [mine, swap_core(mine), beside, swap_core(beside)]

    f_own, f_visited = expert_pass(forward_kernel, f_rows, f_visiting, (), weights, units)
    b_own, b_visited = expert_pass(
        backward_kernel, b_rows, b_visiting, (kept,), weights, 2 * units
    )
    f_out = (f_own + swap_rows_x(f_visited).astype(F32)).astype(BF)
    b_out = (b_own + swap_rows_x(b_visited).astype(F32)).astype(BF)
    f_back = exchange(f_out.reshape(nz, capacity, width)).reshape(-1, width)
    forward_next = to_section(unpack(forward_routes[0], f_back), 1)
    b_moved = to_section(b_out, -1)
    b_back = exchange(b_moved.reshape(nz, capacity, width)).reshape(-1, width)
    pairs = [(i, (i - 1) % 8) for i in range(8)]
    backward_next = unpack(lax.ppermute(backward_routes[0], ("h", "y"), pairs), b_back)
    return forward_next[None], backward_next[None]


def solution(mesh):
    pipes = mesh.shape["pipe"]
    fine = Mesh(mesh.devices.reshape(2, pipes // 2, 8, 4, 2), ("h", "y", "z", "x", "c"))
    pipe, expert = ("h", "y"), ("z", "x", "c")
    tokens = P(pipe, expert, None)
    return jax.shard_map(
        body,
        mesh=fine,
        in_specs=(
            tokens, tokens, tokens, tokens, tokens, tokens,
            P(pipe, None, None, None, expert),
            P(pipe, None, expert),
            P(pipe, None, expert),
            P(pipe, expert, None),
        ),
        out_specs=(tokens, tokens),
        check_vma=False,
    )
```

```python
import jax
import jax.numpy as jnp
from jax import lax
from jax.experimental import pallas as pl
from jax.experimental.pallas import tpu as pltpu
from jax.sharding import Mesh, PartitionSpec as P

BF = jnp.bfloat16
F32 = jnp.float32
ROWS_T = (((1,), (1,)), ((), ()))
COLUMNS = 512
QUARTERS = 4
GATE_COLUMNS = 128
VMEM = pl.BlockSpec(memory_space=pltpu.VMEM)


def permute(block, axis, targets):
    return lax.ppermute(block, axis, list(enumerate(targets)))


def swap_core(block):
    return permute(block, "c", (1, 0))


def swap_weights(block):
    targets = [((x ^ (1 + 2 * c)) * 2 + c) for x in range(4) for c in range(2)]
    return permute(block, ("x", "c"), targets)


def swap_rows(block):
    return permute(block, "x", (2, 3, 0, 1))


def exchange(block):
    return lax.all_to_all(block, "z", split_axis=0, concat_axis=0, tiled=True)


def order_of(routes_row):
    tokens = routes_row.shape[1]
    rows = jax.lax.broadcasted_iota(jnp.int32, (tokens, tokens), 0)
    cols = jax.lax.broadcasted_iota(jnp.int32, (tokens, tokens), 1)
    column = jnp.sum(jnp.where(rows == cols, routes_row, 0), axis=1, keepdims=True)
    same = (column == routes_row).astype(jnp.int32)
    slot_row = jnp.sum(jnp.where(rows < cols, same, 0), axis=0, keepdims=True)
    slot_column = jnp.sum(jnp.where(cols < rows, same, 0), axis=1, keepdims=True)
    return column, slot_column, slot_row, rows, cols


def pack_kernel(f_routes, b_routes, f_gates, b_gates, x, y, out):
    tokens, width = x.shape
    tables, gates = [], []
    for number, (routes, gate) in enumerate(((f_routes, f_gates), (b_routes, b_gates))):
        routes_row, gate_row = routes[...], gate[...].astype(F32)
        _, _, slot_row, rows, cols = order_of(routes_row)
        key = routes_row * 16 + number * 8 + slot_row
        places = jax.lax.broadcasted_iota(jnp.int32, (2 * tokens, tokens), 0)
        tables.append((places == key).astype(F32).astype(BF))
        gate_column = jnp.sum(jnp.where(rows == cols, gate_row, 0.0), axis=1, keepdims=True)
        gates.append(jnp.broadcast_to(gate_column, (tokens, GATE_COLUMNS)).astype(BF))
    for start in range(0, width, COLUMNS):
        at = pl.ds(start, COLUMNS)
        picked = jnp.dot(tables[0], x[:, at], preferred_element_type=F32)
        picked = picked + jnp.dot(tables[1], y[:, at], preferred_element_type=F32)
        out[:, at] = picked.astype(BF)
    picked = jnp.dot(tables[0], gates[0], preferred_element_type=F32)
    picked = picked + jnp.dot(tables[1], gates[1], preferred_element_type=F32)
    out[:, pl.ds(width, GATE_COLUMNS)] = picked.astype(BF)


def pack(f_routes, b_routes, f_gates, b_gates, x, y):
    tokens, width = x.shape
    return pl.pallas_call(
        pack_kernel,
        out_shape=jax.ShapeDtypeStruct((2 * tokens, width + GATE_COLUMNS), BF),
        in_specs=[VMEM] * 6,
        out_specs=VMEM,
        cost_estimate=pl.CostEstimate(
            flops=8 * tokens * tokens * width, bytes_accessed=8 * tokens * width, transcendentals=0
        ),
    )(f_routes, b_routes, f_gates, b_gates, x, y)


def unpack_into(routes, slots, out):
    column, slot_column, _, _, places = order_of(routes[...])
    table = (places == column * 8 + slot_column).astype(F32).astype(BF)
    for q, within, at in column_chunks(out.shape[1]):
        out[:, at] = jnp.dot(table, slots[q, :, within], preferred_element_type=F32).astype(BF)


def unpack_first_kernel(odd, f_routes, b_routes, slots, out):
    @pl.when(odd[0] == 1)
    def _():
        unpack_into(f_routes, slots, out)

    @pl.when(odd[0] == 0)
    def _():
        unpack_into(b_routes, slots, out)


def unpack_second_kernel(odd, f_routes, b_routes, first, slots, f_out, b_out):
    @pl.when(odd[0] == 1)
    def _():
        f_out[...] = first[...]
        unpack_into(b_routes, slots, b_out)

    @pl.when(odd[0] == 0)
    def _():
        b_out[...] = first[...]
        unpack_into(f_routes, slots, f_out)


def unpack(odd, f_routes, b_routes, first, second):
    quarters, tokens, part = first.shape
    width = quarters * part
    rows = jax.ShapeDtypeStruct((tokens, width), BF)
    scalar = pl.BlockSpec(memory_space=pltpu.SMEM)
    cost = pl.CostEstimate(
        flops=2 * tokens * tokens * width, bytes_accessed=4 * tokens * width, transcendentals=0
    )
    done = pl.pallas_call(
        unpack_first_kernel,
        out_shape=rows,
        in_specs=[scalar] + [VMEM] * 3,
        out_specs=VMEM,
        cost_estimate=cost,
    )(odd, f_routes, b_routes, first)
    return pl.pallas_call(
        unpack_second_kernel,
        out_shape=(rows, rows),
        in_specs=[scalar] + [VMEM] * 4,
        out_specs=(VMEM, VMEM),
        cost_estimate=cost,
    )(odd, f_routes, b_routes, done, second)


def spread(quarters):
    return lax.all_to_all(quarters, "y", split_axis=0, concat_axis=0, tiled=True)


def go_home(parts, capacity):
    blocks = jnp.stack(parts).reshape(-1, capacity, parts[0].shape[1])
    homed = lax.all_to_all(blocks, ("y", "z"), split_axis=0, concat_axis=0, tiled=True)
    return homed.reshape(len(parts), -1, blocks.shape[2])


def column_chunks(width):
    quarter = width // QUARTERS
    for q in range(QUARTERS):
        for start in range(0, quarter, COLUMNS):
            size = min(COLUMNS, quarter - start)
            yield q, pl.ds(start, size), pl.ds(q * quarter + start, size)


def load_weights(refs, gate_up, down, sems):
    for u in range(4):
        yield (
            pltpu.make_async_copy(refs[u], gate_up.at[u], sems.at[u]),
            pltpu.make_async_copy(refs[4 + u], down.at[u], sems.at[4 + u]),
        )


def forward_kernel(own, visiting, *refs):
    weights, (out_own, out_visiting, rows, gate_up, down, hidden, sems) = refs[:8], refs[8:]
    copies = list(load_weights(weights, gate_up, down, sems))
    for pair in copies:
        pair[0].start()
        pair[1].start()
    half, width = own.shape[0], rows.shape[1]
    units = down.shape[1]
    gates = [ref[:, pl.ds(width, GATE_COLUMNS)].astype(F32)[:, :1] for ref in (own, visiting)]
    rows[pl.ds(0, half), :] = own[:, pl.ds(0, width)]
    rows[pl.ds(half, half), :] = visiting[:, pl.ds(0, width)]
    for u in range(4):
        copies[u][0].wait()
        pre = jnp.dot(rows[...], gate_up[u], preferred_element_type=F32)
        gate, up = pre[:, :units], pre[:, units:]
        hidden[u] = (gate * jax.nn.sigmoid(gate) * up).astype(BF)
    for u in range(4):
        copies[u][1].wait()
    for q, within, at in column_chunks(width):
        total = jnp.dot(hidden[0], down[0, :, at], preferred_element_type=F32)
        for u in range(1, 4):
            total = total + jnp.dot(hidden[u], down[u, :, at], preferred_element_type=F32)
        out_own[q, :, within] = own[:, at].astype(F32) + gates[0] * total[:half]
        out_visiting[q, :, within] = (gates[1] * total[half:]).astype(BF)


def backward_kernel(own, visiting, saved, *refs):
    weights, (out_own, out_visiting, rows, gate_up, down, grads, sems) = refs[:8], refs[8:]
    copies = list(load_weights(weights, gate_up, down, sems))
    for pair in copies:
        pair[1].start()
        pair[0].start()
    half, width = own.shape[0], rows.shape[1]
    units = down.shape[1]
    for at_row, ref in ((0, own), (half, visiting)):
        gate = ref[:, pl.ds(width, GATE_COLUMNS)].astype(F32)[:, :1]
        for start in range(0, width, COLUMNS):
            at = pl.ds(start, COLUMNS)
            rows[pl.ds(at_row, half), at] = (gate * ref[:, at].astype(F32)).astype(BF)
    for u in range(4):
        copies[u][1].wait()
        grad = lax.dot_general(rows[...], down[u], ROWS_T, preferred_element_type=F32)
        a, b = saved[u, 0].astype(F32), saved[u, 1].astype(F32)
        sig = jax.nn.sigmoid(a)
        grads[u, :, pl.ds(0, units)] = (grad * b * sig * (1.0 + a * (1.0 - sig))).astype(BF)
        grads[u, :, pl.ds(units, units)] = (grad * a * sig).astype(BF)
    for u in range(4):
        copies[u][0].wait()
    for q, within, at in column_chunks(width):
        total = lax.dot_general(grads[0], gate_up[0, at, :], ROWS_T, preferred_element_type=F32)
        for u in range(1, 4):
            total = total + lax.dot_general(
                grads[u], gate_up[u, at, :], ROWS_T, preferred_element_type=F32
            )
        out_own[q, :, within] = own[:, at].astype(F32) + total[:half]
        out_visiting[q, :, within] = total[half:].astype(BF)


def expert_pass(kernel, own, visiting, extra, weights, middle):
    half, units = own.shape[0], weights[4].shape[0]
    width = own.shape[1] - GATE_COLUMNS
    quarters = (QUARTERS, half, width // QUARTERS)
    rows, flops = 2 * half, 2 * 2 * half * width * 4 * units * 3
    return pl.pallas_call(
        kernel,
        out_shape=(jax.ShapeDtypeStruct(quarters, F32), jax.ShapeDtypeStruct(quarters, BF)),
        in_specs=[VMEM] * (2 + len(extra)) + [pl.BlockSpec(memory_space=pl.ANY)] * 8,
        out_specs=(VMEM, VMEM),
        scratch_shapes=[
            pltpu.VMEM((rows, width), BF),
            pltpu.VMEM((4, width, 2 * units), BF),
            pltpu.VMEM((4, units, width), BF),
            pltpu.VMEM((4, rows, middle), BF),
            pltpu.SemaphoreType.DMA((8,)),
        ],
        compiler_params=pltpu.CompilerParams(vmem_limit_bytes=40 * 1024 * 1024),
        cost_estimate=pl.CostEstimate(
            flops=flops, bytes_accessed=12 * width * units * 2 + 5 * half * width * 2, transcendentals=0
        ),
    )(own, visiting, *extra, *weights)


def body(
    forward_state, grad_state, forward_routes, forward_gates, backward_routes, backward_gates,
    saved_preacts, gate_weight, up_weight, down_weight,
):
    x, y, saved = forward_state[0], grad_state[0], saved_preacts[0]
    width = x.shape[1]
    capacity, units = saved.shape[2], saved.shape[3]
    nz, nx, nc = lax.axis_size("z"), lax.axis_size("x"), lax.axis_size("c")
    f_routes, b_routes, f_gates, b_gates = (
        array[0].reshape(1, -1)
        for array in (forward_routes, backward_routes, forward_gates, backward_gates)
    )
    packed = pack(f_routes, b_routes, f_gates, b_gates, x, y)
    packed, gate_here, up_here, down_here = lax.optimization_barrier(
        (packed, gate_weight[0], up_weight[0], down_weight[0])
    )
    arrived = exchange(packed.reshape(nz, 2 * capacity, packed.shape[1]))

    own_weights = [jnp.concatenate([gate_here, up_here], axis=1), down_here]
    beside_weights = [swap_weights(mine) for mine in own_weights]
    across_weights = [swap_core(mine) for mine in own_weights]
    across_weights[0], saved = lax.optimization_barrier((across_weights[0], saved))
    weights = []
    for mine, across, beside in zip(own_weights, across_weights, beside_weights):
        weights += [mine, across, beside, swap_core(beside)]

    me_x, me_c = lax.axis_index("x"), lax.axis_index("c")
    by_place = saved.reshape(2, nz, nx, nc, capacity, units)

    def kept_for(at_x):
        rows_of = [
            lax.dynamic_index_in_dim(by_place, at, 2, keepdims=False) for at in (at_x, at_x ^ 2)
        ]
        return jnp.stack(rows_of, 1)

    here = jnp.stack([kept_for(me_x), swap_weights(kept_for(me_x ^ (1 + 2 * me_c)))])
    mine = lax.dynamic_index_in_dim(here, me_c, 4, keepdims=False)
    theirs = swap_core(lax.dynamic_index_in_dim(here, 1 - me_c, 4, keepdims=False))
    kept = jnp.stack([mine, theirs], 1).reshape(4, 2, 2 * nz * capacity, units)

    f_moved = permute(f_routes, ("h", "y"), [(i + 1) % 8 for i in range(8)])
    b_moved = permute(b_routes, ("h", "y"), [(i - 1) % 8 for i in range(8)])
    arrived, weights, kept = lax.optimization_barrier((arrived, weights, kept))

    f_rows = arrived[:, :capacity].reshape(nz * capacity, -1)
    b_rows = arrived[:, capacity:].reshape(nz * capacity, -1)
    f_own, f_visited = expert_pass(forward_kernel, f_rows, swap_rows(f_rows), (), weights, units)
    b_own, b_visited = expert_pass(
        backward_kernel, b_rows, swap_rows(b_rows), (kept,), weights, 2 * units
    )
    f_out = (f_own + swap_rows(f_visited).astype(F32)).astype(BF)
    b_out = (b_own + swap_rows(b_visited).astype(F32)).astype(BF)
    f_spread, b_spread = spread(f_out), spread(b_out)
    crossed = permute(jnp.stack([f_spread[3], b_spread[0]]), "h", (1, 0))
    first = go_home([b_spread[1], f_spread[0], b_spread[3], f_spread[2]], capacity)
    second = go_home([crossed[0], b_spread[2], f_spread[1], crossed[1]], capacity)
    odd = lax.rem(lax.axis_index("y"), 2).astype(jnp.int32).reshape(1)
    forward_next, backward_next = unpack(odd, f_moved, b_moved, first, second)
    return forward_next[None], backward_next[None]


def solution(mesh):
    pipes = mesh.shape["pipe"]
    fine = Mesh(mesh.devices.reshape(2, pipes // 2, 8, 4, 2), ("h", "y", "z", "x", "c"))
    pipe, expert = ("h", "y"), ("z", "x", "c")
    tokens = P(pipe, expert, None)
    return jax.shard_map(
        body,
        mesh=fine,
        in_specs=(
            tokens, tokens, tokens, tokens, tokens, tokens,
            P(pipe, None, None, None, expert),
            P(pipe, None, expert),
            P(pipe, None, expert),
            P(pipe, expert, None),
        ),
        out_specs=(tokens, tokens),
        check_vma=False,
    )
```

```python
import jax
import jax.numpy as jnp
from jax import lax
from jax.experimental import pallas as pl
from jax.experimental.pallas import tpu as pltpu
from jax.sharding import Mesh, PartitionSpec as P

BF = jnp.bfloat16
F32 = jnp.float32
ROWS_T = (((1,), (1,)), ((), ()))
COLUMNS = 512
QUARTERS = 4
GATE_COLUMNS = 128
VMEM = pl.BlockSpec(memory_space=pltpu.VMEM)


def permute(block, axis, targets):
    return lax.ppermute(block, axis, list(enumerate(targets)))


def swap_core(block):
    return permute(block, "c", (1, 0))


def swap_weights(block):
    targets = [((x ^ (1 + 2 * c)) * 2 + c) for x in range(4) for c in range(2)]
    return permute(block, ("x", "c"), targets)


def swap_rows(block):
    return permute(block, "x", (2, 3, 0, 1))


def exchange(block):
    return lax.all_to_all(block, "z", split_axis=0, concat_axis=0, tiled=True)


def order_of(routes_row):
    tokens = routes_row.shape[1]
    rows = jax.lax.broadcasted_iota(jnp.int32, (tokens, tokens), 0)
    cols = jax.lax.broadcasted_iota(jnp.int32, (tokens, tokens), 1)
    column = jnp.sum(jnp.where(rows == cols, routes_row, 0), axis=1, keepdims=True)
    same = (column == routes_row).astype(jnp.int32)
    slot_row = jnp.sum(jnp.where(rows < cols, same, 0), axis=0, keepdims=True)
    slot_column = jnp.sum(jnp.where(cols < rows, same, 0), axis=1, keepdims=True)
    return column, slot_column, slot_row, rows, cols


def pack_kernel(f_routes, b_routes, f_gates, b_gates, x, y, out):
    tokens, width = x.shape
    tables, gates = [], []
    for number, (routes, gate) in enumerate(((f_routes, f_gates), (b_routes, b_gates))):
        routes_row, gate_row = routes[...], gate[...].astype(F32)
        _, _, slot_row, rows, cols = order_of(routes_row)
        key = routes_row * 16 + number * 8 + slot_row
        places = jax.lax.broadcasted_iota(jnp.int32, (2 * tokens, tokens), 0)
        tables.append((places == key).astype(F32).astype(BF))
        gate_column = jnp.sum(jnp.where(rows == cols, gate_row, 0.0), axis=1, keepdims=True)
        gates.append(jnp.broadcast_to(gate_column, (tokens, GATE_COLUMNS)).astype(BF))
    for start in range(0, width, COLUMNS):
        at = pl.ds(start, COLUMNS)
        picked = jnp.dot(tables[0], x[:, at], preferred_element_type=F32)
        picked = picked + jnp.dot(tables[1], y[:, at], preferred_element_type=F32)
        out[:, at] = picked.astype(BF)
    picked = jnp.dot(tables[0], gates[0], preferred_element_type=F32)
    picked = picked + jnp.dot(tables[1], gates[1], preferred_element_type=F32)
    out[:, pl.ds(width, GATE_COLUMNS)] = picked.astype(BF)


def pack(f_routes, b_routes, f_gates, b_gates, x, y):
    tokens, width = x.shape
    return pl.pallas_call(
        pack_kernel,
        out_shape=jax.ShapeDtypeStruct((2 * tokens, width + GATE_COLUMNS), BF),
        in_specs=[VMEM] * 6,
        out_specs=VMEM,
        cost_estimate=pl.CostEstimate(
            flops=8 * tokens * tokens * width, bytes_accessed=8 * tokens * width, transcendentals=0
        ),
    )(f_routes, b_routes, f_gates, b_gates, x, y)


def unpack_kernel(f_routes, b_routes, slots, f_out, b_out):
    tokens, width = f_out.shape
    for number, (routes, out) in enumerate(((f_routes, f_out), (b_routes, b_out))):
        column, slot_column, _, _, _ = order_of(routes[...])
        places = jax.lax.broadcasted_iota(jnp.int32, (tokens, 2 * tokens), 1)
        table = (places == column * 16 + number * 8 + slot_column).astype(F32).astype(BF)
        for q, within, at in column_chunks(width):
            out[:, at] = jnp.dot(table, slots[q, :, within], preferred_element_type=F32).astype(BF)


def unpack(f_routes, b_routes, slots):
    quarters, tokens, part = slots.shape
    rows = jax.ShapeDtypeStruct((tokens // 2, quarters * part), BF)
    return pl.pallas_call(
        unpack_kernel,
        out_shape=(rows, rows),
        in_specs=[VMEM] * 3,
        out_specs=(VMEM, VMEM),
        cost_estimate=pl.CostEstimate(
            flops=2 * tokens * tokens * quarters * part,
            bytes_accessed=4 * tokens * quarters * part,
            transcendentals=0,
        ),
    )(f_routes, b_routes, slots)


def spread(quarters):
    return lax.all_to_all(quarters, "y", split_axis=0, concat_axis=0, tiled=True)


def go_home(parts, capacity):
    width = parts[0][0].shape[1]
    blocks = [
        jnp.concatenate([rows.reshape(-1, capacity, width) for rows in pair], axis=1) for pair in parts
    ]
    homed = lax.all_to_all(
        jnp.concatenate(blocks), ("y", "z"), split_axis=0, concat_axis=0, tiled=True
    )
    return homed.reshape(len(parts), -1, width)


def column_chunks(width):
    quarter = width // QUARTERS
    for q in range(QUARTERS):
        for start in range(0, quarter, COLUMNS):
            size = min(COLUMNS, quarter - start)
            yield q, pl.ds(start, size), pl.ds(q * quarter + start, size)


def load_weights(refs, gate_up, down, sems):
    for u in range(4):
        yield (
            pltpu.make_async_copy(refs[u], gate_up.at[u], sems.at[u]),
            pltpu.make_async_copy(refs[4 + u], down.at[u], sems.at[4 + u]),
        )


def forward_kernel(own, visiting, *refs):
    weights, (out_own, out_visiting, rows, gate_up, down, hidden, sems) = refs[:8], refs[8:]
    copies = list(load_weights(weights, gate_up, down, sems))
    for pair in copies:
        pair[0].start()
        pair[1].start()
    half, width = own.shape[0], rows.shape[1]
    units = down.shape[1]
    gates = [ref[:, pl.ds(width, GATE_COLUMNS)].astype(F32)[:, :1] for ref in (own, visiting)]
    rows[pl.ds(0, half), :] = own[:, pl.ds(0, width)]
    rows[pl.ds(half, half), :] = visiting[:, pl.ds(0, width)]
    for u in range(4):
        copies[u][0].wait()
        pre = jnp.dot(rows[...], gate_up[u], preferred_element_type=F32)
        gate, up = pre[:, :units], pre[:, units:]
        hidden[u] = (gate * jax.nn.sigmoid(gate) * up).astype(BF)
    for u in range(4):
        copies[u][1].wait()
    for q, within, at in column_chunks(width):
        total = jnp.dot(hidden[0], down[0, :, at], preferred_element_type=F32)
        for u in range(1, 4):
            total = total + jnp.dot(hidden[u], down[u, :, at], preferred_element_type=F32)
        out_own[q, :, within] = own[:, at].astype(F32) + gates[0] * total[:half]
        out_visiting[q, :, within] = (gates[1] * total[half:]).astype(BF)


def backward_kernel(own, visiting, saved, *refs):
    weights, (out_own, out_visiting, rows, gate_up, down, grads, sems) = refs[:8], refs[8:]
    copies = list(load_weights(weights, gate_up, down, sems))
    for pair in copies:
        pair[1].start()
        pair[0].start()
    half, width = own.shape[0], rows.shape[1]
    units = down.shape[1]
    for at_row, ref in ((0, own), (half, visiting)):
        gate = ref[:, pl.ds(width, GATE_COLUMNS)].astype(F32)[:, :1]
        for start in range(0, width, COLUMNS):
            at = pl.ds(start, COLUMNS)
            rows[pl.ds(at_row, half), at] = (gate * ref[:, at].astype(F32)).astype(BF)
    for u in range(4):
        copies[u][1].wait()
        grad = lax.dot_general(rows[...], down[u], ROWS_T, preferred_element_type=F32)
        a, b = saved[u, 0].astype(F32), saved[u, 1].astype(F32)
        sig = jax.nn.sigmoid(a)
        grads[u, :, pl.ds(0, units)] = (grad * b * sig * (1.0 + a * (1.0 - sig))).astype(BF)
        grads[u, :, pl.ds(units, units)] = (grad * a * sig).astype(BF)
    for u in range(4):
        copies[u][0].wait()
    for q, within, at in column_chunks(width):
        total = lax.dot_general(grads[0], gate_up[0, at, :], ROWS_T, preferred_element_type=F32)
        for u in range(1, 4):
            total = total + lax.dot_general(
                grads[u], gate_up[u, at, :], ROWS_T, preferred_element_type=F32
            )
        out_own[q, :, within] = own[:, at].astype(F32) + total[:half]
        out_visiting[q, :, within] = total[half:].astype(BF)


def expert_pass(kernel, own, visiting, extra, weights, middle):
    half, units = own.shape[0], weights[4].shape[0]
    width = own.shape[1] - GATE_COLUMNS
    quarters = (QUARTERS, half, width // QUARTERS)
    rows, flops = 2 * half, 2 * 2 * half * width * 4 * units * 3
    return pl.pallas_call(
        kernel,
        out_shape=(jax.ShapeDtypeStruct(quarters, F32), jax.ShapeDtypeStruct(quarters, BF)),
        in_specs=[VMEM] * (2 + len(extra)) + [pl.BlockSpec(memory_space=pl.ANY)] * 8,
        out_specs=(VMEM, VMEM),
        scratch_shapes=[
            pltpu.VMEM((rows, width), BF),
            pltpu.VMEM((4, width, 2 * units), BF),
            pltpu.VMEM((4, units, width), BF),
            pltpu.VMEM((4, rows, middle), BF),
            pltpu.SemaphoreType.DMA((8,)),
        ],
        compiler_params=pltpu.CompilerParams(vmem_limit_bytes=40 * 1024 * 1024),
        cost_estimate=pl.CostEstimate(
            flops=flops, bytes_accessed=12 * width * units * 2 + 5 * half * width * 2, transcendentals=0
        ),
    )(own, visiting, *extra, *weights)


def body(
    forward_state, grad_state, forward_routes, forward_gates, backward_routes, backward_gates,
    saved_preacts, gate_weight, up_weight, down_weight,
):
    x, y, saved = forward_state[0], grad_state[0], saved_preacts[0]
    width = x.shape[1]
    capacity, units = saved.shape[2], saved.shape[3]
    nz, nx, nc = lax.axis_size("z"), lax.axis_size("x"), lax.axis_size("c")
    f_routes, b_routes, f_gates, b_gates = (
        array[0].reshape(1, -1)
        for array in (forward_routes, backward_routes, forward_gates, backward_gates)
    )
    packed = pack(f_routes, b_routes, f_gates, b_gates, x, y)
    packed, gate_here, up_here, down_here = lax.optimization_barrier(
        (packed, gate_weight[0], up_weight[0], down_weight[0])
    )
    arrived = exchange(packed.reshape(nz, 2 * capacity, packed.shape[1]))

    own_weights = [jnp.concatenate([gate_here, up_here], axis=1), down_here]
    beside_weights = [swap_weights(mine) for mine in own_weights]
    across_weights = [swap_core(mine) for mine in own_weights]
    across_weights[0], saved = lax.optimization_barrier((across_weights[0], saved))
    weights = []
    for mine, across, beside in zip(own_weights, across_weights, beside_weights):
        weights += [mine, across, beside, swap_core(beside)]

    me_x, me_c = lax.axis_index("x"), lax.axis_index("c")
    by_place = saved.reshape(2, nz, nx, nc, capacity, units)

    def kept_for(at_x):
        rows_of = [
            lax.dynamic_index_in_dim(by_place, at, 2, keepdims=False) for at in (at_x, at_x ^ 2)
        ]
        return jnp.stack(rows_of, 1)

    here = jnp.stack([kept_for(me_x), swap_weights(kept_for(me_x ^ (1 + 2 * me_c)))])
    mine = lax.dynamic_index_in_dim(here, me_c, 4, keepdims=False)
    theirs = swap_core(lax.dynamic_index_in_dim(here, 1 - me_c, 4, keepdims=False))
    kept = jnp.stack([mine, theirs], 1).reshape(4, 2, 2 * nz * capacity, units)

    f_moved = permute(f_routes, ("h", "y"), [(i + 1) % 8 for i in range(8)])
    b_moved = permute(b_routes, ("h", "y"), [(i - 1) % 8 for i in range(8)])
    arrived, weights, kept = lax.optimization_barrier((arrived, weights, kept))

    f_rows = arrived[:, :capacity].reshape(nz * capacity, -1)
    b_rows = arrived[:, capacity:].reshape(nz * capacity, -1)
    f_own, f_visited = expert_pass(forward_kernel, f_rows, swap_rows(f_rows), (), weights, units)
    b_own, b_visited = expert_pass(
        backward_kernel, b_rows, swap_rows(b_rows), (kept,), weights, 2 * units
    )
    f_out = (f_own + swap_rows(f_visited).astype(F32)).astype(BF)
    b_out = (b_own + swap_rows(b_visited).astype(F32)).astype(BF)
    f_spread, b_spread = spread(f_out), spread(b_out)
    crossed = [permute(rows, "h", (1, 0)) for rows in (f_spread[3], b_spread[0])]
    home = go_home(
        [
            (crossed[0], b_spread[1]),
            (f_spread[0], b_spread[2]),
            (f_spread[1], b_spread[3]),
            (f_spread[2], crossed[1]),
        ],
        capacity,
    )
    forward_next, backward_next = unpack(f_moved, b_moved, home)
    return forward_next[None], backward_next[None]


def solution(mesh):
    pipes = mesh.shape["pipe"]
    fine = Mesh(mesh.devices.reshape(2, pipes // 2, 8, 4, 2), ("h", "y", "z", "x", "c"))
    pipe, expert = ("h", "y"), ("z", "x", "c")
    tokens = P(pipe, expert, None)
    return jax.shard_map(
        body,
        mesh=fine,
        in_specs=(
            tokens, tokens, tokens, tokens, tokens, tokens,
            P(pipe, None, None, None, expert),
            P(pipe, None, expert),
            P(pipe, None, expert),
            P(pipe, expert, None),
        ),
        out_specs=(tokens, tokens),
        check_vma=False,
    )
```

```python
import jax
import jax.numpy as jnp
from jax import lax
from jax.experimental import pallas as pl
from jax.experimental.pallas import tpu as pltpu
from jax.sharding import Mesh, PartitionSpec as P

BF = jnp.bfloat16
F32 = jnp.float32
ROWS_T = (((1,), (1,)), ((), ()))
COLUMNS = 512
QUARTERS = 4
GATE_COLUMNS = 128
VMEM = pl.BlockSpec(memory_space=pltpu.VMEM)


def permute(block, axis, targets):
    return lax.ppermute(block, axis, list(enumerate(targets)))


def swap_core(block):
    return permute(block, "c", (1, 0))


def swap_weights(block):
    targets = [((x ^ (1 + 2 * c)) * 2 + c) for x in range(4) for c in range(2)]
    return permute(block, ("x", "c"), targets)


def swap_rows(block):
    return permute(block, "x", (2, 3, 0, 1))


def exchange(block):
    return lax.all_to_all(block, "z", split_axis=0, concat_axis=0, tiled=True)


def order_of(routes_row):
    tokens = routes_row.shape[1]
    rows = jax.lax.broadcasted_iota(jnp.int32, (tokens, tokens), 0)
    cols = jax.lax.broadcasted_iota(jnp.int32, (tokens, tokens), 1)
    column = jnp.sum(jnp.where(rows == cols, routes_row, 0), axis=1, keepdims=True)
    same = (column == routes_row).astype(jnp.int32)
    slot_row = jnp.sum(jnp.where(rows < cols, same, 0), axis=0, keepdims=True)
    slot_column = jnp.sum(jnp.where(cols < rows, same, 0), axis=1, keepdims=True)
    return column, slot_column, slot_row, rows, cols


def pack_kernel(f_routes, b_routes, f_gates, b_gates, x, y, out):
    tokens, width = x.shape
    tables, gates = [], []
    for number, (routes, gate) in enumerate(((f_routes, f_gates), (b_routes, b_gates))):
        routes_row, gate_row = routes[...], gate[...].astype(F32)
        _, _, slot_row, rows, cols = order_of(routes_row)
        key = routes_row * 16 + number * 8 + slot_row
        places = jax.lax.broadcasted_iota(jnp.int32, (2 * tokens, tokens), 0)
        tables.append((places == key).astype(F32).astype(BF))
        gate_column = jnp.sum(jnp.where(rows == cols, gate_row, 0.0), axis=1, keepdims=True)
        gates.append(jnp.broadcast_to(gate_column, (tokens, GATE_COLUMNS)).astype(BF))
    for start in range(0, width, COLUMNS):
        at = pl.ds(start, COLUMNS)
        picked = jnp.dot(tables[0], x[:, at], preferred_element_type=F32)
        picked = picked + jnp.dot(tables[1], y[:, at], preferred_element_type=F32)
        out[:, at] = picked.astype(BF)
    picked = jnp.dot(tables[0], gates[0], preferred_element_type=F32)
    picked = picked + jnp.dot(tables[1], gates[1], preferred_element_type=F32)
    out[:, pl.ds(width, GATE_COLUMNS)] = picked.astype(BF)


def pack(f_routes, b_routes, f_gates, b_gates, x, y):
    tokens, width = x.shape
    return pl.pallas_call(
        pack_kernel,
        out_shape=jax.ShapeDtypeStruct((2 * tokens, width + GATE_COLUMNS), BF),
        in_specs=[VMEM] * 6,
        out_specs=VMEM,
        cost_estimate=pl.CostEstimate(
            flops=8 * tokens * tokens * width, bytes_accessed=8 * tokens * width, transcendentals=0
        ),
    )(f_routes, b_routes, f_gates, b_gates, x, y)


def unpack_kernel(f_routes, b_routes, slots, f_out, b_out):
    tokens, width = f_out.shape
    for number, (routes, out) in enumerate(((f_routes, f_out), (b_routes, b_out))):
        column, slot_column, _, _, _ = order_of(routes[...])
        places = jax.lax.broadcasted_iota(jnp.int32, (tokens, 2 * tokens), 1)
        table = (places == column * 16 + number * 8 + slot_column).astype(F32).astype(BF)
        for q, within, at in column_chunks(width):
            out[:, at] = jnp.dot(table, slots[q, :, within], preferred_element_type=F32).astype(BF)


def unpack(f_routes, b_routes, slots):
    quarters, tokens, part = slots.shape
    rows = jax.ShapeDtypeStruct((tokens // 2, quarters * part), BF)
    return pl.pallas_call(
        unpack_kernel,
        out_shape=(rows, rows),
        in_specs=[VMEM] * 3,
        out_specs=(VMEM, VMEM),
        cost_estimate=pl.CostEstimate(
            flops=2 * tokens * tokens * quarters * part,
            bytes_accessed=4 * tokens * quarters * part,
            transcendentals=0,
        ),
    )(f_routes, b_routes, slots)


def spread(quarters):
    return lax.all_to_all(quarters, "y", split_axis=0, concat_axis=0, tiled=True)


def go_home(parts, capacity):
    width = parts[0][0].shape[1]
    blocks = [
        jnp.concatenate([rows.reshape(-1, capacity, width) for rows in pair], axis=1) for pair in parts
    ]
    homed = lax.all_to_all(
        jnp.concatenate(blocks), ("y", "z"), split_axis=0, concat_axis=0, tiled=True
    )
    return homed.reshape(len(parts), -1, width)


def column_chunks(width):
    quarter = width // QUARTERS
    for q in range(QUARTERS):
        for start in range(0, quarter, COLUMNS):
            size = min(COLUMNS, quarter - start)
            yield q, pl.ds(start, size), pl.ds(q * quarter + start, size)


def load_weights(refs, gate_up, down, sems):
    for u in range(4):
        yield (
            pltpu.make_async_copy(refs[u], gate_up.at[u], sems.at[u]),
            pltpu.make_async_copy(refs[4 + u], down.at[u], sems.at[4 + u]),
        )


def forward_kernel(own, visiting, *refs):
    weights, (out_own, out_visiting, rows, gate_up, down, hidden, sems) = refs[:8], refs[8:]
    copies = list(load_weights(weights, gate_up, down, sems))
    for pair in copies:
        pair[0].start()
        pair[1].start()
    half, width = own.shape[0], rows.shape[1]
    units = down.shape[1]
    gates = [ref[:, pl.ds(width, GATE_COLUMNS)].astype(F32)[:, :1] for ref in (own, visiting)]
    rows[pl.ds(0, half), :] = own[:, pl.ds(0, width)]
    rows[pl.ds(half, half), :] = visiting[:, pl.ds(0, width)]
    for u in range(4):
        copies[u][0].wait()
        pre = jnp.dot(rows[...], gate_up[u], preferred_element_type=F32)
        gate, up = pre[:, :units], pre[:, units:]
        hidden[u] = (gate * jax.nn.sigmoid(gate) * up).astype(BF)
    for u in range(4):
        copies[u][1].wait()
    for q, within, at in column_chunks(width):
        total = jnp.dot(hidden[0], down[0, :, at], preferred_element_type=F32)
        for u in range(1, 4):
            total = total + jnp.dot(hidden[u], down[u, :, at], preferred_element_type=F32)
        out_own[q, :, within] = own[:, at].astype(F32) + gates[0] * total[:half]
        out_visiting[q, :, within] = (gates[1] * total[half:]).astype(BF)


def backward_kernel(own, visiting, saved, *refs):
    weights, (out_own, out_visiting, rows, gate_up, down, grads, sems) = refs[:8], refs[8:]
    copies = list(load_weights(weights, gate_up, down, sems))
    for pair in copies:
        pair[1].start()
        pair[0].start()
    half, width = own.shape[0], rows.shape[1]
    units = down.shape[1]
    for at_row, ref in ((0, own), (half, visiting)):
        gate = ref[:, pl.ds(width, GATE_COLUMNS)].astype(F32)[:, :1]
        for start in range(0, width, COLUMNS):
            at = pl.ds(start, COLUMNS)
            rows[pl.ds(at_row, half), at] = (gate * ref[:, at].astype(F32)).astype(BF)
    for u in range(4):
        copies[u][1].wait()
        grad = lax.dot_general(rows[...], down[u], ROWS_T, preferred_element_type=F32)
        a, b = saved[u, 0].astype(F32), saved[u, 1].astype(F32)
        sig = jax.nn.sigmoid(a)
        grads[u, :, pl.ds(0, units)] = (grad * b * sig * (1.0 + a * (1.0 - sig))).astype(BF)
        grads[u, :, pl.ds(units, units)] = (grad * a * sig).astype(BF)
    for u in range(4):
        copies[u][0].wait()
    for q, within, at in column_chunks(width):
        total = lax.dot_general(grads[0], gate_up[0, at, :], ROWS_T, preferred_element_type=F32)
        for u in range(1, 4):
            total = total + lax.dot_general(
                grads[u], gate_up[u, at, :], ROWS_T, preferred_element_type=F32
            )
        out_own[q, :, within] = own[:, at].astype(F32) + total[:half]
        out_visiting[q, :, within] = total[half:].astype(BF)


def expert_pass(kernel, own, visiting, extra, weights, middle):
    half, units = own.shape[0], weights[4].shape[0]
    width = own.shape[1] - GATE_COLUMNS
    quarters = (QUARTERS, half, width // QUARTERS)
    rows, flops = 2 * half, 2 * 2 * half * width * 4 * units * 3
    return pl.pallas_call(
        kernel,
        out_shape=(jax.ShapeDtypeStruct(quarters, F32), jax.ShapeDtypeStruct(quarters, BF)),
        in_specs=[VMEM] * (2 + len(extra)) + [pl.BlockSpec(memory_space=pl.ANY)] * 8,
        out_specs=(VMEM, VMEM),
        scratch_shapes=[
            pltpu.VMEM((rows, width), BF),
            pltpu.VMEM((4, width, 2 * units), BF),
            pltpu.VMEM((4, units, width), BF),
            pltpu.VMEM((4, rows, middle), BF),
            pltpu.SemaphoreType.DMA((8,)),
        ],
        compiler_params=pltpu.CompilerParams(vmem_limit_bytes=40 * 1024 * 1024),
        cost_estimate=pl.CostEstimate(
            flops=flops, bytes_accessed=12 * width * units * 2 + 5 * half * width * 2, transcendentals=0
        ),
    )(own, visiting, *extra, *weights)


def body(
    forward_state, grad_state, forward_routes, forward_gates, backward_routes, backward_gates,
    saved_preacts, gate_weight, up_weight, down_weight,
):
    x, y, saved = forward_state[0], grad_state[0], saved_preacts[0]
    width = x.shape[1]
    capacity, units = saved.shape[2], saved.shape[3]
    nz, nx, nc = lax.axis_size("z"), lax.axis_size("x"), lax.axis_size("c")
    f_routes, b_routes, f_gates, b_gates = (
        array[0].reshape(1, -1)
        for array in (forward_routes, backward_routes, forward_gates, backward_gates)
    )
    packed = pack(f_routes, b_routes, f_gates, b_gates, x, y)
    packed, gate_here, up_here, down_here = lax.optimization_barrier(
        (packed, gate_weight[0], up_weight[0], down_weight[0])
    )
    arrived = exchange(packed.reshape(nz, 2 * capacity, packed.shape[1]))

    own_weights = [jnp.concatenate([gate_here, up_here], axis=1), down_here]
    beside_weights = [swap_weights(mine) for mine in own_weights]
    across_weights = [swap_core(mine) for mine in own_weights]
    across_weights[1], saved = lax.optimization_barrier((across_weights[1], saved))
    weights = []
    for mine, across, beside in zip(own_weights, across_weights, beside_weights):
        weights += [mine, across, beside, swap_core(beside)]

    me_x, me_c = lax.axis_index("x"), lax.axis_index("c")
    by_place = saved.reshape(2, nz, nx, nc, capacity, units)

    def kept_for(at_x):
        rows_of = [
            lax.dynamic_index_in_dim(by_place, at, 2, keepdims=False) for at in (at_x, at_x ^ 2)
        ]
        return jnp.stack(rows_of, 1)

    here = jnp.stack([kept_for(me_x), swap_weights(kept_for(me_x ^ (1 + 2 * me_c)))])
    mine = lax.dynamic_index_in_dim(here, me_c, 4, keepdims=False)
    theirs = swap_core(lax.dynamic_index_in_dim(here, 1 - me_c, 4, keepdims=False))
    kept = jnp.stack([mine, theirs], 1).reshape(4, 2, 2 * nz * capacity, units)

    f_moved = permute(f_routes, ("h", "y"), [(i + 1) % 8 for i in range(8)])
    b_moved = permute(b_routes, ("h", "y"), [(i - 1) % 8 for i in range(8)])
    arrived, across_weights[0], kept = lax.optimization_barrier((arrived, across_weights[0], kept))

    f_rows = arrived[:, :capacity].reshape(nz * capacity, -1)
    b_rows = arrived[:, capacity:].reshape(nz * capacity, -1)
    f_own, f_visited = expert_pass(forward_kernel, f_rows, swap_rows(f_rows), (), weights, units)
    b_own, b_visited = expert_pass(
        backward_kernel, b_rows, swap_rows(b_rows), (kept,), weights, 2 * units
    )
    f_out = (f_own + swap_rows(f_visited).astype(F32)).astype(BF)
    b_out = (b_own + swap_rows(b_visited).astype(F32)).astype(BF)
    f_spread, b_spread = spread(f_out), spread(b_out)
    crossed = [permute(rows, "h", (1, 0)) for rows in (f_spread[3], b_spread[0])]
    home = go_home(
        [
            (crossed[0], b_spread[1]),
            (f_spread[0], b_spread[2]),
            (f_spread[1], b_spread[3]),
            (f_spread[2], crossed[1]),
        ],
        capacity,
    )
    forward_next, backward_next = unpack(f_moved, b_moved, home)
    return forward_next[None], backward_next[None]


def solution(mesh):
    pipes = mesh.shape["pipe"]
    fine = Mesh(mesh.devices.reshape(2, pipes // 2, 8, 4, 2), ("h", "y", "z", "x", "c"))
    pipe, expert = ("h", "y"), ("z", "x", "c")
    tokens = P(pipe, expert, None)
    return jax.shard_map(
        body,
        mesh=fine,
        in_specs=(
            tokens, tokens, tokens, tokens, tokens, tokens,
            P(pipe, None, None, None, expert),
            P(pipe, None, expert),
            P(pipe, None, expert),
            P(pipe, expert, None),
        ),
        out_specs=(tokens, tokens),
        check_vma=False,
    )
```

```python
import jax
import jax.numpy as jnp
from jax import lax
from jax.experimental import pallas as pl
from jax.experimental.pallas import tpu as pltpu
from jax.sharding import Mesh, PartitionSpec as P

BF = jnp.bfloat16
F32 = jnp.float32
ROWS_T = (((1,), (1,)), ((), ()))
COLUMNS = 512
QUARTERS = 4
GATE_COLUMNS = 128
VMEM = pl.BlockSpec(memory_space=pltpu.VMEM)


def permute(block, axis, targets):
    return lax.ppermute(block, axis, list(enumerate(targets)))


def swap_core(block):
    return permute(block, "c", (1, 0))


def swap_weights(block):
    targets = [((x ^ (1 + 2 * c)) * 2 + c) for x in range(4) for c in range(2)]
    return permute(block, ("x", "c"), targets)


def swap_rows(block):
    return permute(block, "x", (2, 3, 0, 1))


def exchange(block):
    return lax.all_to_all(block, "z", split_axis=0, concat_axis=0, tiled=True)


def order_of(routes_row):
    tokens = routes_row.shape[1]
    rows = jax.lax.broadcasted_iota(jnp.int32, (tokens, tokens), 0)
    cols = jax.lax.broadcasted_iota(jnp.int32, (tokens, tokens), 1)
    column = jnp.sum(jnp.where(rows == cols, routes_row, 0), axis=1, keepdims=True)
    same = (column == routes_row).astype(jnp.int32)
    slot_row = jnp.sum(jnp.where(rows < cols, same, 0), axis=0, keepdims=True)
    slot_column = jnp.sum(jnp.where(cols < rows, same, 0), axis=1, keepdims=True)
    return column, slot_column, slot_row, rows, cols


def pack_kernel(f_routes, b_routes, f_gates, b_gates, x, y, out):
    tokens, width = x.shape
    tables, gates = [], []
    for number, (routes, gate) in enumerate(((f_routes, f_gates), (b_routes, b_gates))):
        routes_row, gate_row = routes[...], gate[...].astype(F32)
        _, _, slot_row, rows, cols = order_of(routes_row)
        key = routes_row * 16 + number * 8 + slot_row
        places = jax.lax.broadcasted_iota(jnp.int32, (2 * tokens, tokens), 0)
        tables.append((places == key).astype(F32).astype(BF))
        gate_column = jnp.sum(jnp.where(rows == cols, gate_row, 0.0), axis=1, keepdims=True)
        gates.append(jnp.broadcast_to(gate_column, (tokens, GATE_COLUMNS)).astype(BF))
    for start in range(0, width, COLUMNS):
        at = pl.ds(start, COLUMNS)
        picked = jnp.dot(tables[0], x[:, at], preferred_element_type=F32)
        picked = picked + jnp.dot(tables[1], y[:, at], preferred_element_type=F32)
        out[:, at] = picked.astype(BF)
    picked = jnp.dot(tables[0], gates[0], preferred_element_type=F32)
    picked = picked + jnp.dot(tables[1], gates[1], preferred_element_type=F32)
    out[:, pl.ds(width, GATE_COLUMNS)] = picked.astype(BF)


def pack(f_routes, b_routes, f_gates, b_gates, x, y):
    tokens, width = x.shape
    return pl.pallas_call(
        pack_kernel,
        out_shape=jax.ShapeDtypeStruct((2 * tokens, width + GATE_COLUMNS), BF),
        in_specs=[VMEM] * 6,
        out_specs=VMEM,
        cost_estimate=pl.CostEstimate(
            flops=8 * tokens * tokens * width, bytes_accessed=8 * tokens * width, transcendentals=0
        ),
    )(f_routes, b_routes, f_gates, b_gates, x, y)


def unpack_kernel(f_routes, b_routes, slots, f_out, b_out):
    tokens, width = f_out.shape
    for number, (routes, out) in enumerate(((f_routes, f_out), (b_routes, b_out))):
        column, slot_column, _, _, _ = order_of(routes[...])
        places = jax.lax.broadcasted_iota(jnp.int32, (tokens, 2 * tokens), 1)
        table = (places == column * 16 + number * 8 + slot_column).astype(F32).astype(BF)
        for q, within, at in column_chunks(width):
            out[:, at] = jnp.dot(table, slots[q, :, within], preferred_element_type=F32).astype(BF)


def unpack(f_routes, b_routes, slots):
    quarters, tokens, part = slots.shape
    rows = jax.ShapeDtypeStruct((tokens // 2, quarters * part), BF)
    return pl.pallas_call(
        unpack_kernel,
        out_shape=(rows, rows),
        in_specs=[VMEM] * 3,
        out_specs=(VMEM, VMEM),
        cost_estimate=pl.CostEstimate(
            flops=2 * tokens * tokens * quarters * part,
            bytes_accessed=4 * tokens * quarters * part,
            transcendentals=0,
        ),
    )(f_routes, b_routes, slots)


def spread(quarters):
    return lax.all_to_all(quarters, "y", split_axis=0, concat_axis=0, tiled=True)


def go_home(parts, capacity):
    width = parts[0][0].shape[1]
    blocks = [
        jnp.concatenate([rows.reshape(-1, capacity, width) for rows in pair], axis=1) for pair in parts
    ]
    homed = lax.all_to_all(
        jnp.concatenate(blocks), ("y", "z"), split_axis=0, concat_axis=0, tiled=True
    )
    return homed.reshape(len(parts), -1, width)


def column_chunks(width):
    quarter = width // QUARTERS
    for q in range(QUARTERS):
        for start in range(0, quarter, COLUMNS):
            size = min(COLUMNS, quarter - start)
            yield q, pl.ds(start, size), pl.ds(q * quarter + start, size)


def load_weights(refs, gate_up, down, sems):
    units = down.shape[0] // 4
    for u in range(4):
        yield (
            pltpu.make_async_copy(refs[u], gate_up.at[u], sems.at[u]),
            pltpu.make_async_copy(refs[4 + u], down.at[pl.ds(u * units, units), :], sems.at[4 + u]),
        )


def forward_kernel(own, visiting, *refs):
    weights, (out_own, out_visiting, rows, gate_up, down, hidden, sems) = refs[:8], refs[8:]
    copies = list(load_weights(weights, gate_up, down, sems))
    for kind in (0, 1):
        for pair in copies:
            pair[kind].start()
    half, width = own.shape[0], rows.shape[1]
    units = down.shape[0] // 4
    gates = [ref[:, pl.ds(width, GATE_COLUMNS)].astype(F32)[:, :1] for ref in (own, visiting)]
    rows[pl.ds(0, half), :] = own[:, pl.ds(0, width)]
    rows[pl.ds(half, half), :] = visiting[:, pl.ds(0, width)]
    for u in range(4):
        copies[u][0].wait()
        pre = jnp.dot(rows[...], gate_up[u], preferred_element_type=F32)
        gate, up = pre[:, :units], pre[:, units:]
        hidden[:, pl.ds(u * units, units)] = (gate * jax.nn.sigmoid(gate) * up).astype(BF)
    for u in range(4):
        copies[u][1].wait()
    for q, within, at in column_chunks(width):
        total = jnp.dot(hidden[...], down[:, at], preferred_element_type=F32)
        out_own[q, :, within] = own[:, at].astype(F32) + gates[0] * total[:half]
        out_visiting[q, :, within] = (gates[1] * total[half:]).astype(BF)


def backward_kernel(own, visiting, saved, *refs):
    weights, (out_own, out_visiting, rows, gate_up, down, grads, sems) = refs[:8], refs[8:]
    copies = list(load_weights(weights, gate_up, down, sems))
    for kind in (1, 0):
        for pair in copies:
            pair[kind].start()
    half, width = own.shape[0], rows.shape[1]
    units = down.shape[0] // 4
    for at_row, ref in ((0, own), (half, visiting)):
        gate = ref[:, pl.ds(width, GATE_COLUMNS)].astype(F32)[:, :1]
        for start in range(0, width, COLUMNS):
            at = pl.ds(start, COLUMNS)
            rows[pl.ds(at_row, half), at] = (gate * ref[:, at].astype(F32)).astype(BF)
    for u in range(4):
        copies[u][1].wait()
    hidden_grad = lax.dot_general(rows[...], down[...], ROWS_T, preferred_element_type=F32)
    for u in range(4):
        grad = hidden_grad[:, u * units : (u + 1) * units]
        a, b = saved[u, 0].astype(F32), saved[u, 1].astype(F32)
        sig = jax.nn.sigmoid(a)
        grads[u, :, pl.ds(0, units)] = (grad * b * sig * (1.0 + a * (1.0 - sig))).astype(BF)
        grads[u, :, pl.ds(units, units)] = (grad * a * sig).astype(BF)
    for u in range(4):
        copies[u][0].wait()
    for q, within, at in column_chunks(width):
        total = lax.dot_general(grads[0], gate_up[0, at, :], ROWS_T, preferred_element_type=F32)
        for u in range(1, 4):
            total = total + lax.dot_general(
                grads[u], gate_up[u, at, :], ROWS_T, preferred_element_type=F32
            )
        out_own[q, :, within] = own[:, at].astype(F32) + total[:half]
        out_visiting[q, :, within] = total[half:].astype(BF)


def expert_pass(kernel, own, visiting, extra, weights, middle):
    half, units = own.shape[0], weights[4].shape[0]
    width = own.shape[1] - GATE_COLUMNS
    quarters = (QUARTERS, half, width // QUARTERS)
    rows, flops = 2 * half, 2 * 2 * half * width * 4 * units * 3
    return pl.pallas_call(
        kernel,
        out_shape=(jax.ShapeDtypeStruct(quarters, F32), jax.ShapeDtypeStruct(quarters, BF)),
        in_specs=[VMEM] * (2 + len(extra)) + [pl.BlockSpec(memory_space=pl.ANY)] * 8,
        out_specs=(VMEM, VMEM),
        scratch_shapes=[
            pltpu.VMEM((rows, width), BF),
            pltpu.VMEM((4, width, 2 * units), BF),
            pltpu.VMEM((4 * units, width), BF),
            pltpu.VMEM(middle, BF),
            pltpu.SemaphoreType.DMA((8,)),
        ],
        compiler_params=pltpu.CompilerParams(vmem_limit_bytes=40 * 1024 * 1024),
        cost_estimate=pl.CostEstimate(
            flops=flops, bytes_accessed=12 * width * units * 2 + 5 * half * width * 2, transcendentals=0
        ),
    )(own, visiting, *extra, *weights)


def body(
    forward_state, grad_state, forward_routes, forward_gates, backward_routes, backward_gates,
    saved_preacts, gate_weight, up_weight, down_weight,
):
    x, y, saved = forward_state[0], grad_state[0], saved_preacts[0]
    width = x.shape[1]
    capacity, units = saved.shape[2], saved.shape[3]
    nz, nx, nc = lax.axis_size("z"), lax.axis_size("x"), lax.axis_size("c")
    f_routes, b_routes, f_gates, b_gates = (
        array[0].reshape(1, -1)
        for array in (forward_routes, backward_routes, forward_gates, backward_gates)
    )
    packed = pack(f_routes, b_routes, f_gates, b_gates, x, y)
    packed, gate_here, up_here, down_here = lax.optimization_barrier(
        (packed, gate_weight[0], up_weight[0], down_weight[0])
    )
    arrived = exchange(packed.reshape(nz, 2 * capacity, packed.shape[1]))

    own_weights = [jnp.concatenate([gate_here, up_here], axis=1), down_here]
    beside_weights = [swap_weights(mine) for mine in own_weights]
    across_weights = [swap_core(mine) for mine in own_weights]
    across_weights[1], saved = lax.optimization_barrier((across_weights[1], saved))
    weights = []
    for mine, across, beside in zip(own_weights, across_weights, beside_weights):
        weights += [mine, across, beside, swap_core(beside)]

    me_x, me_c = lax.axis_index("x"), lax.axis_index("c")
    by_place = saved.reshape(2, nz, nx, nc, capacity, units)

    def kept_for(at_x):
        rows_of = [
            lax.dynamic_index_in_dim(by_place, at, 2, keepdims=False) for at in (at_x, at_x ^ 2)
        ]
        return jnp.stack(rows_of, 1)

    here = jnp.stack([kept_for(me_x), swap_weights(kept_for(me_x ^ (1 + 2 * me_c)))])
    mine = lax.dynamic_index_in_dim(here, me_c, 4, keepdims=False)
    theirs = swap_core(lax.dynamic_index_in_dim(here, 1 - me_c, 4, keepdims=False))
    kept = jnp.stack([mine, theirs], 1).reshape(4, 2, 2 * nz * capacity, units)

    f_moved = permute(f_routes, ("h", "y"), [(i + 1) % 8 for i in range(8)])
    b_moved = permute(b_routes, ("h", "y"), [(i - 1) % 8 for i in range(8)])
    arrived, across_weights[0], kept = lax.optimization_barrier((arrived, across_weights[0], kept))

    f_rows = arrived[:, :capacity].reshape(nz * capacity, -1)
    b_rows = arrived[:, capacity:].reshape(nz * capacity, -1)
    b_own, b_visited = expert_pass(
        backward_kernel, b_rows, swap_rows(b_rows), (kept,), weights, (4, 2 * nz * capacity, 2 * units)
    )
    b_own, f_visiting = lax.optimization_barrier((b_own, swap_rows(f_rows)))
    f_own, f_visited = expert_pass(
        forward_kernel, f_rows, f_visiting, (), weights, (2 * nz * capacity, 4 * units)
    )
    f_out = (f_own + swap_rows(f_visited).astype(F32)).astype(BF)
    b_out = (b_own + swap_rows(b_visited).astype(F32)).astype(BF)
    f_spread, b_spread = spread(f_out), spread(b_out)
    crossed = [permute(rows, "h", (1, 0)) for rows in (f_spread[3], b_spread[0])]
    home = go_home(
        [
            (crossed[0], b_spread[1]),
            (f_spread[0], b_spread[2]),
            (f_spread[1], b_spread[3]),
            (f_spread[2], crossed[1]),
        ],
        capacity,
    )
    forward_next, backward_next = unpack(f_moved, b_moved, home)
    return forward_next[None], backward_next[None]


def solution(mesh):
    pipes = mesh.shape["pipe"]
    fine = Mesh(mesh.devices.reshape(2, pipes // 2, 8, 4, 2), ("h", "y", "z", "x", "c"))
    pipe, expert = ("h", "y"), ("z", "x", "c")
    tokens = P(pipe, expert, None)
    return jax.shard_map(
        body,
        mesh=fine,
        in_specs=(
            tokens, tokens, tokens, tokens, tokens, tokens,
            P(pipe, None, None, None, expert),
            P(pipe, None, expert),
            P(pipe, None, expert),
            P(pipe, expert, None),
        ),
        out_specs=(tokens, tokens),
        check_vma=False,
    )
```
